32 devices in a mesh: grp: 1, dap: 32 (over z, y, x, core), sub: 1.
Axes of the slice: x: 2, y: 2, z: 4, core: 2. Of those that a mesh axis runs over, the one named last changes fastest.
Arguments:
- homolog_embedding: bfloat16 [32, 128, 256], P(('grp', 'sub'), 'dap'), may hold values from -6 to 6
- alignment_mask: int32 [32, 128], P(('grp', 'sub'), 'dap'), may hold values from 0 to 1, as said below
- pair_activation: bfloat16 [128, 128, 128], P(('grp', 'dap'), 'sub'), may hold values from -6 to 6
- sequence_mask: int32 [128], P('grp'), may hold values from 0 to 1, as said below
- homolog_scaling_factor: float32 [256], replicated, may hold values from 0.1 to 1.9
- homolog_mapping_matrix: bfloat16 [256, 64], replicated, may hold values from -0.375 to 0.375
- outer_output_weight: bfloat16 [1024, 128], replicated, may hold values from -0.5 to 0.5
- outer_output_bias: float32 [128], replicated, may hold values from -3 to 3
- pair_norm_gains: float32 [4, 128], replicated, may hold values from 0.1 to 1.9
- triangle_input_weights: bfloat16 [2, 128, 640], replicated, may hold values from -0.5 to 0.5
- triangle_output_weights: bfloat16 [2, 128, 128], replicated, may hold values from -0.5 to 0.5
Outputs:
- pair_out: bfloat16 [128, 128, 128], P(('grp', 'dap'), 'sub')
The draws below stay inside these ranges and needn't reach their ends.
Inputs may be any that keep to these rules, and one draw needn't show every extreme that they name: `sequence_mask`: 1 on the first residues of the crop and 0 on the rest; between 1 and 32 residues are padding. `alignment_mask`: 0 wherever sequence_mask is 0.
All inputs are finite; a program needn't handle non-finite values.
Results may differ from the reference program's by a relative error of at most 0.017.
Values may be sent and summed in bfloat16 or wider, within the bound.
A program may use at most 64 MiB of HBM per device.

```python
import jax
import jax.numpy as jnp
from jax import lax

SEQUENCER_DEPTH = 256
C = 128
TENSOR_DEPTH = 32
AMINO_NUMBER = 128
HOMOLOG_NUMBER = 32


def crop_length(key):
    return AMINO_NUMBER - jax.random.randint(key, (), 1, AMINO_NUMBER // 4 + 1)


def draw_sequence_mask(key, part):
    length = crop_length(key)
    return (jnp.arange(AMINO_NUMBER) < length).astype(jnp.int32)


def draw_alignment_mask(key, part):
    length = crop_length(key)
    key = jax.random.fold_in(key, 9)
    retained = jax.random.randint(key, (HOMOLOG_NUMBER, AMINO_NUMBER), 0, 4) > 0
    inside = jnp.arange(AMINO_NUMBER)[None, :] < length
    return jnp.where(retained & inside, 1, 0).astype(jnp.int32)


def block_scale(rng, dims, cuts, least, largest):
    def one(position, parts):
        draws = jax.random.uniform(jax.random.fold_in(jax.random.fold_in(rng, 6), position), (parts,), jnp.float32, least / len(cuts), largest / len(cuts))
        return jnp.repeat(jnp.exp(draws), dims[position] // parts).reshape((-1,) + (1,) * (len(dims) - position - 1))

    gain = one(*cuts[0])
    for cut in cuts[1:]:
        gain = gain * one(*cut)
    return gain


def noise(rng, dims, scale, bound, shards=(), dtype=jnp.bfloat16):
    values = jax.random.normal(rng, dims, jnp.float32) * scale
    if len(shards) > 0:
        values = block_scale(rng, dims, shards, -0.22, 0.18) * values
    return jnp.clip(values, min=-bound, max=bound).astype(dtype)


def setup_inputs(seed: int = 0, part: int = 0) -> dict:
    keys = jax.random.split(jax.random.key(seed), 12)
    part_keys = jax.random.split(jax.random.fold_in(keys[11], part), 12)
    homolog_embedding = noise(part_keys[0], (HOMOLOG_NUMBER, AMINO_NUMBER, SEQUENCER_DEPTH), 1.0, 6.0, ((1, 32),))
    alignment_mask = draw_alignment_mask(jax.random.fold_in(jax.random.fold_in(keys[11], part), 71), part)
    pair_activation = noise(part_keys[2], (AMINO_NUMBER, AMINO_NUMBER, C), 1.0, 6.0, ((0, 32),))
    sequence_mask = draw_sequence_mask(jax.random.fold_in(jax.random.fold_in(keys[11], part), 71), part)
    homolog_scaling_factor = jnp.clip(1.0 + 0.18 * jax.random.normal(keys[4], (SEQUENCER_DEPTH,), jnp.float32), 0.1, 1.9)
    homolog_mapping_matrix = noise(keys[5], (SEQUENCER_DEPTH, 2 * TENSOR_DEPTH), SEQUENCER_DEPTH ** -0.5, 0.375)
    outer_output_weight = noise(keys[6], (TENSOR_DEPTH * TENSOR_DEPTH, C), C ** -0.5, 0.5)
    outer_output_bias = noise(keys[7], (C,), 0.5, 3.0, (), jnp.float32)
    pair_norm_gains = jnp.clip(1.0 + 0.18 * jax.random.normal(keys[8], (4, C), jnp.float32), 0.1, 1.9)
    triangle_input_weights = noise(keys[9], (2, C, 5 * C), C ** -0.5, 0.5)
    triangle_output_weights = noise(keys[10], (2, C, C), C ** -0.5, 0.5)
    return {"homolog_embedding": homolog_embedding, "alignment_mask": alignment_mask, "pair_activation": pair_activation, "sequence_mask": sequence_mask, "homolog_scaling_factor": homolog_scaling_factor, "homolog_mapping_matrix": homolog_mapping_matrix, "outer_output_weight": outer_output_weight, "outer_output_bias": outer_output_bias, "pair_norm_gains": pair_norm_gains, "triangle_input_weights": triangle_input_weights, "triangle_output_weights": triangle_output_weights}


def apply_layer_norm(values, norm_gain, dimension):
    center = values - lax.optimization_barrier(jnp.mean(values, dimension, keepdims=True))
    spread = lax.optimization_barrier(jnp.mean(center * center, dimension, keepdims=True))
    return center * lax.rsqrt(spread + 1e-05) * norm_gain

def triangle(current, pair_mask, norm_in, norm_out, weight_in, weight_out, outgoing):

    def project_row(packed):
        pair_row, mask_row = packed
        normed = apply_layer_norm(pair_row.astype(jnp.float32), norm_in, -1).astype(jnp.bfloat16)
        projected_alignment = jnp.dot(normed, weight_in, preferred_element_type=jnp.float32)
        left_value, right_value, left_gate, right_gate, output_gate = jnp.split(projected_alignment, 5, axis=1)
        left_side = (mask_row[:, None] * jax.nn.sigmoid(left_gate) * left_value).astype(jnp.bfloat16)
        right_side = (mask_row[:, None] * jax.nn.sigmoid(right_gate) * right_value).astype(jnp.bfloat16)
        return (left_side.T, right_side.T, jax.nn.sigmoid(output_gate).T)
    left_side, right_side, gating = lax.map(project_row, (current, pair_mask))
    left_side = jnp.transpose(left_side, (1, 0, 2))
    right_side = jnp.transpose(right_side, (1, 0, 2))

    def channel(packed):
        first_side, second_side = packed
        if outgoing:
            return jnp.dot(first_side, second_side.T, preferred_element_type=jnp.float32).astype(jnp.bfloat16)
        return jnp.dot(first_side.T, second_side, preferred_element_type=jnp.float32).astype(jnp.bfloat16)
    mixed = lax.map(channel, (left_side, right_side))
    mixed = jnp.transpose(mixed, (1, 0, 2))

    def finish_row(packed):
        pair_row, mixed_row, gate_row = packed
        normed = apply_layer_norm(mixed_row.T.astype(jnp.float32), norm_out, -1).astype(jnp.bfloat16)
        update = jnp.dot(normed, weight_out, preferred_element_type=jnp.float32)
        return (pair_row.astype(jnp.float32) + gate_row.T * update).astype(jnp.bfloat16)
    return lax.map(finish_row, (current, mixed, gating))

def reference(homolog_embedding, alignment_mask, pair_activation, sequence_mask, homolog_scaling_factor, homolog_mapping_matrix, outer_output_weight, outer_output_bias, pair_norm_gains, triangle_input_weights, triangle_output_weights):
    alignment_normed = apply_layer_norm(homolog_embedding.astype(jnp.float32), homolog_scaling_factor, -1).astype(jnp.bfloat16)
    mask_as_float = alignment_mask.astype(jnp.float32)
    projected_alignment = jnp.einsum('ftv,vy->fty', alignment_normed.astype(jnp.float32), homolog_mapping_matrix.astype(jnp.float32)) * mask_as_float[:, :, None]
    left_proj = projected_alignment[:, :, :TENSOR_DEPTH].astype(jnp.bfloat16)
    right_proj = projected_alignment[:, :, TENSOR_DEPTH:].astype(jnp.bfloat16)
    counts = jnp.dot(mask_as_float.T, mask_as_float, preferred_element_type=jnp.float32)
    right_wide = right_proj.astype(jnp.float32)

    def opm_row(packed):
        left_row, count_row, pair_row = packed
        outer_prod = jnp.einsum('sp,sjq->jpq', left_row, right_wide).astype(jnp.bfloat16).reshape(AMINO_NUMBER, TENSOR_DEPTH * TENSOR_DEPTH)
        values = jnp.dot(outer_prod, outer_output_weight, preferred_element_type=jnp.float32) + outer_output_bias
        return (pair_row.astype(jnp.float32) + values / jnp.maximum(count_row, 1.0)[:, None]).astype(jnp.bfloat16)
    current = lax.map(opm_row, (jnp.transpose(left_proj.astype(jnp.float32), (1, 0, 2)), counts, pair_activation))
    seq_float = sequence_mask.astype(jnp.float32)
    pair_mask = seq_float[:, None] * seq_float[None, :]
    for which in range(2):
        current = triangle(current, pair_mask, pair_norm_gains[2 * which], pair_norm_gains[2 * which + 1], triangle_input_weights[which], triangle_output_weights[which], which == 0)
    return current
```

```python
import jax
import jax.numpy as jnp
from jax import lax
from jax.sharding import PartitionSpec as P


def apply_layer_norm(values, norm_gain, dimension):
    center = values - jnp.mean(values, dimension, keepdims=True)
    spread = jnp.mean(center * center, dimension, keepdims=True)
    return center * lax.rsqrt(spread + 1e-05) * norm_gain


def triangle(current, pair_mask, norm_in, norm_out, weight_in, weight_out, outgoing):
    width = weight_out.shape[0]
    normed = apply_layer_norm(current.astype(jnp.float32), norm_in, 2).astype(jnp.bfloat16)
    projected_alignment = jnp.einsum(
        "rhk,kc->crh", normed, weight_in, preferred_element_type=jnp.float32
    )
    left_value = projected_alignment[:width]
    right_value = projected_alignment[width : 2 * width]
    left_gate = projected_alignment[2 * width : 3 * width]
    right_gate = projected_alignment[3 * width : 4 * width]
    gating = jax.nn.sigmoid(projected_alignment[4 * width :])
    left_side = (pair_mask[None] * jax.nn.sigmoid(left_gate) * left_value).astype(jnp.bfloat16)
    right_side = (pair_mask[None] * jax.nn.sigmoid(right_gate) * right_value).astype(jnp.bfloat16)
    both_sides = lax.all_to_all(
        jnp.stack([left_side, right_side], axis=1), "dap", split_axis=0, concat_axis=2, tiled=True
    )
    left_channels, right_channels = both_sides[:, 0], both_sides[:, 1]
    if outgoing:
        left_full = lax.all_gather(left_channels, "sub", axis=2, tiled=True)
        right_rows = lax.all_to_all(right_channels, "sub", split_axis=1, concat_axis=2, tiled=True)
        mixed = jnp.einsum(
            "cik,cjk->cij", left_full, right_rows, preferred_element_type=jnp.float32
        )
    else:
        left_full = lax.all_gather(left_channels, "sub", axis=2, tiled=True)
        mixed = jnp.einsum(
            "cki,ckj->cij", left_full, right_channels, preferred_element_type=jnp.float32
        )
    returned = lax.all_to_all(
        mixed.astype(jnp.bfloat16), "dap", split_axis=1, concat_axis=0, tiled=True
    )
    mixed_norm = apply_layer_norm(returned.astype(jnp.float32), norm_out[:, None, None], 0).astype(
        jnp.bfloat16
    )
    update = jnp.einsum("crh,cd->drh", mixed_norm, weight_out, preferred_element_type=jnp.float32)
    return (current.astype(jnp.float32) + jnp.transpose(gating * update, (1, 2, 0))).astype(
        jnp.bfloat16
    )


def local(
    homolog_embedding,
    alignment_mask,
    pair_activation,
    sequence_mask,
    homolog_scaling_factor,
    homolog_mapping_matrix,
    outer_output_weight,
    outer_output_bias,
    pair_norm_gains,
    triangle_input_weights,
    triangle_output_weights,
):
    outer_product_width = homolog_mapping_matrix.shape[1] // 2
    alignment_row_count = pair_activation.shape[0]
    column_halfway = pair_activation.shape[1]
    row_halfway = homolog_embedding.shape[0]
    dap_index = lax.axis_index("dap")
    sub_index = lax.axis_index("sub")
    alignment_normed = apply_layer_norm(
        homolog_embedding.astype(jnp.float32), homolog_scaling_factor, 2
    ).astype(jnp.bfloat16)
    mask_as_float = alignment_mask.astype(jnp.float32)
    projected_alignment = (
        jnp.einsum(
            "ftv,vy->fty",
            alignment_normed,
            homolog_mapping_matrix,
            preferred_element_type=jnp.float32,
        )
        * mask_as_float[:, :, None]
    )
    left_proj = (
        projected_alignment[:, :, :outer_product_width]
        .astype(jnp.bfloat16)
        .reshape(row_halfway, alignment_row_count * outer_product_width)
    )
    right_proj = (
        projected_alignment[:, :, outer_product_width:]
        .astype(jnp.bfloat16)
        .reshape(row_halfway, alignment_row_count * outer_product_width)
    )
    mask_bits = mask_as_float.astype(jnp.bfloat16)
    left_complete, right_all, mask_all = (
        lax.all_gather(left_proj, "sub", axis=0, tiled=True),
        lax.all_gather(right_proj, "sub", axis=0, tiled=True),
        lax.all_gather(mask_bits, "sub", axis=0, tiled=True),
    )
    packed = jnp.concatenate([right_all, mask_all], axis=1)
    copies = jnp.broadcast_to(packed[None], (lax.axis_size("dap"),) + packed.shape)
    arrived = lax.all_to_all(copies, "dap", split_axis=0, concat_axis=0, tiled=True)
    arrived = jnp.transpose(arrived, (1, 0, 2))
    right_columns = right_all.shape[1]
    right_wide = arrived[:, :, :right_columns].reshape(arrived.shape[0], -1)
    mask_wide = arrived[:, :, right_columns:].reshape(arrived.shape[0], -1)
    right_column_block = lax.dynamic_slice_in_dim(
        right_wide,
        sub_index * (column_halfway * outer_product_width),
        column_halfway * outer_product_width,
        1,
    )
    mask_cols = lax.dynamic_slice_in_dim(mask_wide, sub_index * column_halfway, column_halfway, 1)
    alignment_mask_total = left_complete.shape[0]
    left_row_block = jnp.transpose(
        left_complete.reshape(alignment_mask_total, alignment_row_count, outer_product_width),
        (1, 0, 2),
    )
    right_value_grid = right_column_block.reshape(
        alignment_mask_total, column_halfway, outer_product_width
    )
    counts = jnp.dot(mask_all.T, mask_cols, preferred_element_type=jnp.float32)

    def opm_row(packed):
        left_row, count_row, pair_row = packed
        outer_prod = jnp.einsum(
            "sp,shq->hpq", left_row, right_value_grid, preferred_element_type=jnp.float32
        )
        outer_prod = outer_prod.astype(jnp.bfloat16).reshape(
            column_halfway, outer_product_width * outer_product_width
        )
        values = (
            jnp.dot(outer_prod, outer_output_weight, preferred_element_type=jnp.float32)
            + outer_output_bias
        )
        return (
            pair_row.astype(jnp.float32) + values / jnp.maximum(count_row, 1.0)[:, None]
        ).astype(jnp.bfloat16)

    current = lax.map(opm_row, (left_row_block, counts, pair_activation))
    seq_float = sequence_mask.astype(jnp.float32)
    row_mask = lax.dynamic_slice_in_dim(
        seq_float, dap_index * alignment_row_count, alignment_row_count
    )
    col_mask = lax.dynamic_slice_in_dim(seq_float, sub_index * column_halfway, column_halfway)
    pair_mask = row_mask[:, None] * col_mask[None, :]
    for which in range(2):
        current = triangle(
            current,
            pair_mask,
            pair_norm_gains[2 * which],
            pair_norm_gains[2 * which + 1],
            triangle_input_weights[which],
            triangle_output_weights[which],
            which == 0,
        )
    return current


def solution(mesh):
    return jax.shard_map(
        local,
        mesh=mesh,
        in_specs=(
            P(("grp", "sub"), "dap", None),
            P(("grp", "sub"), "dap"),
            P(("grp", "dap"), "sub", None),
            P("grp"),
            P(),
            P(),
            P(),
            P(),
            P(),
            P(),
            P(),
        ),
        out_specs=P(("grp", "dap"), "sub", None),
        check_vma=False,
    )
```

```python
import functools

import jax
import jax.numpy as jnp
from jax import lax
from jax.experimental import pallas as pl
from jax.experimental.pallas import tpu as pltpu
from jax.sharding import PartitionSpec as P


def apply_layer_norm(values, norm_gain, dimension):
    center = values - jnp.mean(values, dimension, keepdims=True)
    spread = jnp.mean(center * center, dimension, keepdims=True)
    return center * lax.rsqrt(spread + 1e-05) * norm_gain


def triangle(current, pair_mask, norm_in, norm_out, weight_in, weight_out, outgoing):
    width = weight_out.shape[0]
    normed = apply_layer_norm(current.astype(jnp.float32), norm_in, 2).astype(jnp.bfloat16)
    projected_alignment = jnp.einsum(
        "rhk,kc->crh", normed, weight_in, preferred_element_type=jnp.float32
    )
    left_value = projected_alignment[:width]
    right_value = projected_alignment[width : 2 * width]
    left_gate = projected_alignment[2 * width : 3 * width]
    right_gate = projected_alignment[3 * width : 4 * width]
    gating = jax.nn.sigmoid(projected_alignment[4 * width :])
    left_side = (pair_mask[None] * jax.nn.sigmoid(left_gate) * left_value).astype(jnp.bfloat16)
    right_side = (pair_mask[None] * jax.nn.sigmoid(right_gate) * right_value).astype(jnp.bfloat16)
    both_sides = lax.all_to_all(
        jnp.stack([left_side, right_side], axis=1), "dap", split_axis=0, concat_axis=2, tiled=True
    )
    left_channels, right_channels = both_sides[:, 0], both_sides[:, 1]
    if outgoing:
        left_full = lax.all_gather(left_channels, "sub", axis=2, tiled=True)
        right_rows = lax.all_to_all(right_channels, "sub", split_axis=1, concat_axis=2, tiled=True)
        mixed = jnp.einsum(
            "cik,cjk->cij", left_full, right_rows, preferred_element_type=jnp.float32
        )
    else:
        left_full = lax.all_gather(left_channels, "sub", axis=2, tiled=True)
        mixed = jnp.einsum(
            "cki,ckj->cij", left_full, right_channels, preferred_element_type=jnp.float32
        )
    returned = lax.all_to_all(
        mixed.astype(jnp.bfloat16), "dap", split_axis=1, concat_axis=0, tiled=True
    )
    mixed_norm = apply_layer_norm(returned.astype(jnp.float32), norm_out[:, None, None], 0).astype(
        jnp.bfloat16
    )
    update = jnp.einsum("crh,cd->drh", mixed_norm, weight_out, preferred_element_type=jnp.float32)
    return (current.astype(jnp.float32) + jnp.transpose(gating * update, (1, 2, 0))).astype(
        jnp.bfloat16
    )


def local(
    homolog_embedding,
    alignment_mask,
    pair_activation,
    sequence_mask,
    homolog_scaling_factor,
    homolog_mapping_matrix,
    outer_output_weight,
    outer_output_bias,
    pair_norm_gains,
    triangle_input_weights,
    triangle_output_weights,
):
    outer_product_width = homolog_mapping_matrix.shape[1] // 2
    alignment_row_count = pair_activation.shape[0]
    column_halfway = pair_activation.shape[1]
    row_halfway = homolog_embedding.shape[0]
    dap_index = lax.axis_index("dap")
    sub_index = lax.axis_index("sub")
    alignment_normed = apply_layer_norm(
        homolog_embedding.astype(jnp.float32), homolog_scaling_factor, 2
    ).astype(jnp.bfloat16)
    mask_as_float = alignment_mask.astype(jnp.float32)
    projected_alignment = (
        jnp.einsum(
            "ftv,vy->fty",
            alignment_normed,
            homolog_mapping_matrix,
            preferred_element_type=jnp.float32,
        )
        * mask_as_float[:, :, None]
    )
    left_proj = (
        projected_alignment[:, :, :outer_product_width]
        .astype(jnp.bfloat16)
        .reshape(row_halfway, alignment_row_count * outer_product_width)
    )
    right_proj = (
        projected_alignment[:, :, outer_product_width:]
        .astype(jnp.bfloat16)
        .reshape(row_halfway, alignment_row_count * outer_product_width)
    )
    mask_bits = mask_as_float.astype(jnp.bfloat16)
    left_complete, right_all, mask_all = (
        lax.all_gather(left_proj, "sub", axis=0, tiled=True),
        lax.all_gather(right_proj, "sub", axis=0, tiled=True),
        lax.all_gather(mask_bits, "sub", axis=0, tiled=True),
    )
    packed = jnp.concatenate([right_all, mask_all], axis=1)
    copies = jnp.broadcast_to(packed[None], (lax.axis_size("dap"),) + packed.shape)
    arrived = lax.all_to_all(copies, "dap", split_axis=0, concat_axis=0, tiled=True)
    arrived = jnp.transpose(arrived, (1, 0, 2))
    right_columns = right_all.shape[1]
    right_wide = arrived[:, :, :right_columns].reshape(arrived.shape[0], -1)
    mask_wide = arrived[:, :, right_columns:].reshape(arrived.shape[0], -1)
    right_column_block = lax.dynamic_slice_in_dim(
        right_wide,
        sub_index * (column_halfway * outer_product_width),
        column_halfway * outer_product_width,
        1,
    )
    mask_cols = lax.dynamic_slice_in_dim(mask_wide, sub_index * column_halfway, column_halfway, 1)
    alignment_mask_total = left_complete.shape[0]
    left_row_block = jnp.transpose(
        left_complete.reshape(alignment_mask_total, alignment_row_count, outer_product_width),
        (1, 0, 2),
    )
    right_value_grid = right_column_block.reshape(
        alignment_mask_total, column_halfway, outer_product_width
    )
    counts = jnp.dot(mask_all.T, mask_cols, preferred_element_type=jnp.float32)

    def opm_row(packed):
        left_row, count_row, pair_row = packed
        outer_prod = jnp.einsum(
            "sp,shq->hpq", left_row, right_value_grid, preferred_element_type=jnp.float32
        )
        outer_prod = outer_prod.astype(jnp.bfloat16).reshape(
            column_halfway, outer_product_width * outer_product_width
        )
        values = (
            jnp.dot(outer_prod, outer_output_weight, preferred_element_type=jnp.float32)
            + outer_output_bias
        )
        return (
            pair_row.astype(jnp.float32) + values / jnp.maximum(count_row, 1.0)[:, None]
        ).astype(jnp.bfloat16)

    current = lax.map(opm_row, (left_row_block, counts, pair_activation))
    seq_float = sequence_mask.astype(jnp.float32)
    row_mask = lax.dynamic_slice_in_dim(
        seq_float, dap_index * alignment_row_count, alignment_row_count
    )
    col_mask = lax.dynamic_slice_in_dim(seq_float, sub_index * column_halfway, column_halfway)
    pair_mask = row_mask[:, None] * col_mask[None, :]
    for which in range(2):
        current = triangle(
            current,
            pair_mask,
            pair_norm_gains[2 * which],
            pair_norm_gains[2 * which + 1],
            triangle_input_weights[which],
            triangle_output_weights[which],
            which == 0,
        )
    return current


F32, BF16 = jnp.float32, jnp.bfloat16
MESH = pl.DeviceIdType.MESH
LANES = 128


def dot(a, b, da, db):
    return lax.dot_general(a, b, (((da,), (db,)), ((), ())), preferred_element_type=F32)


def exchange(n, me, source, arrived, send_sem, recv_sem):
    def start(offset, carry):
        peer = lax.rem(me + offset, n)
        pltpu.make_async_remote_copy(
            src_ref=source(peer),
            dst_ref=arrived.at[me],
            send_sem=send_sem,
            recv_sem=recv_sem,
            device_id={"dap": peer},
            device_id_type=MESH,
        ).start()
        return carry

    lax.fori_loop(1, n, start, 0)


def await_bytes(n, arrived, sem):
    others = arrived.at[pl.ds(0, n - 1)]
    pltpu.make_async_copy(others, others, sem).wait()


def fused_kernel(
    n,
    rows,
    depth,
    x_ref,
    mask_ref,
    pair_ref,
    seq_ref,
    scale_ref,
    map_ref,
    outer_ref,
    bias_ref,
    gains_ref,
    w_in_ref,
    w_out_ref,
    out_ref,
    send_a,
    recv_a,
    send_b,
    recv_b,
    send_c,
    recv_c,
    wide,
    first,
    second,
    mixed_rows,
    factors,
    w_turned,
    sems,
):
    me = lax.axis_index("dap")
    barrier = pltpu.get_barrier_semaphore()

    def greet(offset, carry):
        pl.semaphore_signal(
            barrier, inc=1, device_id={"dap": lax.rem(me + offset, n)}, device_id_type=MESH
        )
        return carry

    lax.fori_loop(1, n, greet, 0)

    width = pair_ref.shape[2]
    tensor = map_ref.shape[1] // 2
    per = width // n
    strip = rows * per
    blocks = tensor * depth // LANES
    high = tensor // blocks

    normed = apply_layer_norm(x_ref[...].astype(F32), scale_ref[...], 1).astype(BF16)
    mask_col = mask_ref[...].astype(F32)
    proj = dot(normed, map_ref[...], 1, 0) * mask_col
    left = proj[:, :tensor].astype(BF16)
    turned = jnp.concatenate(
        [proj, jnp.broadcast_to(mask_col, (rows * depth, LANES - 2 * tensor))], axis=1
    ).T
    pieces = []
    for j in range(rows):
        lanes = slice(j * depth, (j + 1) * depth)
        pieces.append(
            jnp.concatenate(
                [
                    turned[tensor + h * blocks : tensor + (h + 1) * blocks, lanes]
                    for h in range(high)
                ],
                axis=1,
            )
        )
    row_of = lax.broadcasted_iota(jnp.int32, (4 * rows, depth), 0) // 4
    mask_rows = jnp.zeros((4 * rows, depth), F32)
    for j in range(rows):
        spread = turned[2 * tensor : 2 * tensor + 4 * rows, j * depth : (j + 1) * depth]
        mask_rows = jnp.where(row_of == j, spread, mask_rows)
    mask_rows = jnp.concatenate([mask_rows, jnp.zeros((4 * rows, LANES - depth), F32)], axis=1)
    packed = jnp.concatenate(pieces + [mask_rows], axis=0).astype(BF16)
    send_a[...] = packed
    recv_a[me] = packed
    pl.semaphore_wait(barrier, n - 1)
    exchange(n, me, lambda peer: send_a, recv_a, sems.at[0], sems.at[1])

    wide[...] = outer_ref[...].astype(F32)
    for q in range(tensor):
        weight = wide[pl.ds(q, tensor, stride=tensor), :].astype(BF16)
        factor = dot(left, weight, 1, 0).astype(BF16)
        place = (q % blocks) * LANES + (q // blocks) * depth
        for i in range(rows):
            factors[place : place + depth, i * width : (i + 1) * width] = factor[
                i * depth : (i + 1) * depth
            ]
    for t in range(2):
        w_turned[t] = w_in_ref[t, :, : 4 * width].astype(F32).T.astype(BF16)
    seq = seq_ref[...].astype(F32)
    lane = lax.broadcasted_iota(jnp.int32, seq.shape, 1)
    pair_mask = jnp.concatenate(
        [
            seq * jnp.sum(jnp.where(lane == me * rows + r, seq, 0.0), 1, keepdims=True)
            for r in range(rows)
        ],
        axis=1,
    )

    await_bytes(n, recv_a, sems.at[1])
    total = n * rows
    kept = rows * blocks
    wide[...] = recv_a[:, :kept, :].astype(F32).reshape(n * kept, LANES)
    first[...] = recv_a[:, kept:, :].astype(F32).reshape(4 * total, LANES)
    right = jnp.concatenate(
        [wide[pl.ds(b, total, stride=blocks), :].astype(BF16) for b in range(blocks)], axis=1
    )
    mask_all = first[pl.ds(0, total, stride=4), :][:, :depth].astype(BF16)
    values = dot(right, factors[...], 1, 0)
    current = []
    for i in range(rows):
        own = jnp.broadcast_to(mask_col[i * depth : (i + 1) * depth], (depth, width)).astype(BF16)
        counts = dot(mask_all, own, 1, 0)
        update = (values[:, i * width : (i + 1) * width] + bias_ref[...]) / jnp.maximum(counts, 1.0)
        current.append((pair_ref[i].astype(F32) + update).astype(BF16))

    for t in range(2):
        z = jnp.concatenate([row.astype(F32) for row in current], axis=0)
        normed = apply_layer_norm(z, gains_ref[2 * t : 2 * t + 1, :], 1).astype(BF16)
        turned = dot(w_turned[t], normed, 1, 1)
        for side, scratch in ((0, first), (1, second)):
            value = turned[side * width : (side + 1) * width]
            gate = turned[(2 + side) * width : (3 + side) * width]
            gated = pair_mask * jax.nn.sigmoid(gate) * value
            for r in range(rows):
                scratch[r * width : (r + 1) * width, :] = gated[:, r * total : (r + 1) * total]
        for d in range(n):
            send_b[t, d, :strip, :] = first[pl.ds(d, strip, stride=n), :].astype(BF16)
            send_b[t, d, strip:, :] = second[pl.ds(d, strip, stride=n), :].astype(BF16)
        s = 2 + 4 * t
        exchange(n, me, lambda peer: send_b.at[t, peer], recv_b.at[t], sems.at[s], sems.at[s + 1])
        recv_b[t, me] = send_b[t, me]
        gating = jax.nn.sigmoid(dot(normed, w_in_ref[t, :, 4 * width :], 1, 0))
        gain = jnp.broadcast_to(gains_ref[2 * t + 1 : 2 * t + 2, :], (total, width)).T
        await_bytes(n, recv_b.at[t], sems.at[s + 1])
        first[...] = recv_b[t, :, :strip, :].astype(F32).reshape(n * strip, LANES)
        second[...] = recv_b[t, :, strip:, :].astype(F32).reshape(n * strip, LANES)
        for c in range(per):
            one = first[pl.ds(c, total, stride=per), :].astype(BF16)
            two = second[pl.ds(c, total, stride=per), :].astype(BF16)
            over = 1 - t
            mixed_rows[pl.ds(c, total, stride=per), :] = dot(one, two, over, over)
        send_c[t] = mixed_rows[...].astype(BF16).reshape(n, strip, LANES)
        exchange(n, me, lambda peer: send_c.at[t, peer], recv_c.at[t], sems.at[s + 2], sems.at[s + 3])
        recv_c[t, me] = send_c[t, me]
        await_bytes(n, recv_c.at[t], sems.at[s + 3])
        first[...] = recv_c[t].astype(F32).reshape(n * strip, LANES)
        following = []
        for r in range(rows):
            mixed = jnp.concatenate(
                [first[pl.ds(r * per + c, n, stride=strip), :] for c in range(per)], axis=0
            )
            mixed_norm = apply_layer_norm(mixed, gain, 0).astype(BF16)
            update = dot(mixed_norm, w_out_ref[t], 0, 0)
            block = slice(r * total, (r + 1) * total)
            following.append((z[block] + gating[block] * update).astype(BF16))
        current = following
    for r in range(rows):
        out_ref[r] = current[r]
    await_bytes(n, recv_a, sems.at[0])
    for t in range(2):
        await_bytes(n, recv_b.at[t], sems.at[2 + 4 * t])
        await_bytes(n, recv_c.at[t], sems.at[4 + 4 * t])


def fused(
    n,
    homolog_embedding,
    alignment_mask,
    pair_activation,
    sequence_mask,
    homolog_scaling_factor,
    homolog_mapping_matrix,
    outer_output_weight,
    outer_output_bias,
    pair_norm_gains,
    triangle_input_weights,
    triangle_output_weights,
):
    depth, rows, channels = homolog_embedding.shape
    total, width = pair_activation.shape[1:]
    strip = rows * (width // n)
    outer = outer_output_weight.shape[0]
    kept = rows * (homolog_mapping_matrix.shape[1] // 2) * depth // LANES
    vmem = pl.BlockSpec(memory_space=pltpu.VMEM)
    return pl.pallas_call(
        functools.partial(fused_kernel, n, rows, depth),
        out_shape=jax.ShapeDtypeStruct(pair_activation.shape, BF16),
        in_specs=[vmem] * 11,
        out_specs=vmem,
        scratch_shapes=[
            pltpu.VMEM((kept + 4 * rows, LANES), BF16),
            pltpu.VMEM((n, kept + 4 * rows, LANES), BF16),
            pltpu.VMEM((2, n, 2 * strip, total), BF16),
            pltpu.VMEM((2, n, 2 * strip, total), BF16),
            pltpu.VMEM((2, n, strip, total), BF16),
            pltpu.VMEM((2, n, strip, total), BF16),
            pltpu.VMEM((outer, width), F32),
            pltpu.VMEM((rows * width, LANES), F32),
            pltpu.VMEM((rows * width, LANES), F32),
            pltpu.VMEM((rows * width, LANES), F32),
            pltpu.VMEM((outer, rows * width), BF16),
            pltpu.VMEM((2, 4 * width, width), BF16),
            pltpu.SemaphoreType.DMA((10,)),
        ],
        compiler_params=pltpu.CompilerParams(
            collective_id=0, has_side_effects=True, vmem_limit_bytes=40 * 1024 * 1024
        ),
    )(
        jnp.transpose(homolog_embedding, (1, 0, 2)).reshape(rows * depth, channels),
        jnp.transpose(alignment_mask).reshape(rows * depth, 1),
        pair_activation,
        sequence_mask.reshape(1, total),
        homolog_scaling_factor.reshape(1, channels),
        homolog_mapping_matrix,
        outer_output_weight,
        outer_output_bias.reshape(1, width),
        pair_norm_gains,
        triangle_input_weights,
        triangle_output_weights,
    )


def solution(mesh):
    n, sub = mesh.shape["dap"], mesh.shape["sub"]

    def chosen(*arrays):
        depth, rows, _ = arrays[0].shape
        total, width = arrays[2].shape[1:]
        tensor = arrays[5].shape[1] // 2
        fits = (
            sub == 1
            and (depth, rows, total, width, tensor) == (32, 4, LANES, LANES, 32)
            and n * rows == total
        )
        return fused(n, *arrays) if fits else local(*arrays)
    return jax.shard_map(
        chosen,
        mesh=mesh,
        in_specs=(
            P(("grp", "sub"), "dap", None),
            P(("grp", "sub"), "dap"),
            P(("grp", "dap"), "sub", None),
            P("grp"),
            P(),
            P(),
            P(),
            P(),
            P(),
            P(),
            P(),
        ),
        out_specs=P(("grp", "dap"), "sub", None),
        check_vma=False,
    )
```

```python
import functools

import jax
import jax.numpy as jnp
from jax import lax
from jax.experimental import pallas as pl
from jax.experimental.pallas import tpu as pltpu
from jax.sharding import PartitionSpec as P


def apply_layer_norm(values, norm_gain, dimension):
    center = values - jnp.mean(values, dimension, keepdims=True)
    spread = jnp.mean(center * center, dimension, keepdims=True)
    return center * lax.rsqrt(spread + 1e-05) * norm_gain


def triangle(current, pair_mask, norm_in, norm_out, weight_in, weight_out, outgoing):
    width = weight_out.shape[0]
    normed = apply_layer_norm(current.astype(jnp.float32), norm_in, 2).astype(jnp.bfloat16)
    projected_alignment = jnp.einsum(
        "rhk,kc->crh", normed, weight_in, preferred_element_type=jnp.float32
    )
    left_value = projected_alignment[:width]
    right_value = projected_alignment[width : 2 * width]
    left_gate = projected_alignment[2 * width : 3 * width]
    right_gate = projected_alignment[3 * width : 4 * width]
    gating = jax.nn.sigmoid(projected_alignment[4 * width :])
    left_side = (pair_mask[None] * jax.nn.sigmoid(left_gate) * left_value).astype(jnp.bfloat16)
    right_side = (pair_mask[None] * jax.nn.sigmoid(right_gate) * right_value).astype(jnp.bfloat16)
    both_sides = lax.all_to_all(
        jnp.stack([left_side, right_side], axis=1), "dap", split_axis=0, concat_axis=2, tiled=True
    )
    left_channels, right_channels = both_sides[:, 0], both_sides[:, 1]
    if outgoing:
        left_full = lax.all_gather(left_channels, "sub", axis=2, tiled=True)
        right_rows = lax.all_to_all(right_channels, "sub", split_axis=1, concat_axis=2, tiled=True)
        mixed = jnp.einsum(
            "cik,cjk->cij", left_full, right_rows, preferred_element_type=jnp.float32
        )
    else:
        left_full = lax.all_gather(left_channels, "sub", axis=2, tiled=True)
        mixed = jnp.einsum(
            "cki,ckj->cij", left_full, right_channels, preferred_element_type=jnp.float32
        )
    returned = lax.all_to_all(
        mixed.astype(jnp.bfloat16), "dap", split_axis=1, concat_axis=0, tiled=True
    )
    mixed_norm = apply_layer_norm(returned.astype(jnp.float32), norm_out[:, None, None], 0).astype(
        jnp.bfloat16
    )
    update = jnp.einsum("crh,cd->drh", mixed_norm, weight_out, preferred_element_type=jnp.float32)
    return (current.astype(jnp.float32) + jnp.transpose(gating * update, (1, 2, 0))).astype(
        jnp.bfloat16
    )


def local(
    homolog_embedding,
    alignment_mask,
    pair_activation,
    sequence_mask,
    homolog_scaling_factor,
    homolog_mapping_matrix,
    outer_output_weight,
    outer_output_bias,
    pair_norm_gains,
    triangle_input_weights,
    triangle_output_weights,
):
    outer_product_width = homolog_mapping_matrix.shape[1] // 2
    alignment_row_count = pair_activation.shape[0]
    column_halfway = pair_activation.shape[1]
    row_halfway = homolog_embedding.shape[0]
    dap_index = lax.axis_index("dap")
    sub_index = lax.axis_index("sub")
    alignment_normed = apply_layer_norm(
        homolog_embedding.astype(jnp.float32), homolog_scaling_factor, 2
    ).astype(jnp.bfloat16)
    mask_as_float = alignment_mask.astype(jnp.float32)
    projected_alignment = (
        jnp.einsum(
            "ftv,vy->fty",
            alignment_normed,
            homolog_mapping_matrix,
            preferred_element_type=jnp.float32,
        )
        * mask_as_float[:, :, None]
    )
    left_proj = (
        projected_alignment[:, :, :outer_product_width]
        .astype(jnp.bfloat16)
        .reshape(row_halfway, alignment_row_count * outer_product_width)
    )
    right_proj = (
        projected_alignment[:, :, outer_product_width:]
        .astype(jnp.bfloat16)
        .reshape(row_halfway, alignment_row_count * outer_product_width)
    )
    mask_bits = mask_as_float.astype(jnp.bfloat16)
    left_complete, right_all, mask_all = (
        lax.all_gather(left_proj, "sub", axis=0, tiled=True),
        lax.all_gather(right_proj, "sub", axis=0, tiled=True),
        lax.all_gather(mask_bits, "sub", axis=0, tiled=True),
    )
    packed = jnp.concatenate([right_all, mask_all], axis=1)
    copies = jnp.broadcast_to(packed[None], (lax.axis_size("dap"),) + packed.shape)
    arrived = lax.all_to_all(copies, "dap", split_axis=0, concat_axis=0, tiled=True)
    arrived = jnp.transpose(arrived, (1, 0, 2))
    right_columns = right_all.shape[1]
    right_wide = arrived[:, :, :right_columns].reshape(arrived.shape[0], -1)
    mask_wide = arrived[:, :, right_columns:].reshape(arrived.shape[0], -1)
    right_column_block = lax.dynamic_slice_in_dim(
        right_wide,
        sub_index * (column_halfway * outer_product_width),
        column_halfway * outer_product_width,
        1,
    )
    mask_cols = lax.dynamic_slice_in_dim(mask_wide, sub_index * column_halfway, column_halfway, 1)
    alignment_mask_total = left_complete.shape[0]
    left_row_block = jnp.transpose(
        left_complete.reshape(alignment_mask_total, alignment_row_count, outer_product_width),
        (1, 0, 2),
    )
    right_value_grid = right_column_block.reshape(
        alignment_mask_total, column_halfway, outer_product_width
    )
    counts = jnp.dot(mask_all.T, mask_cols, preferred_element_type=jnp.float32)

    def opm_row(packed):
        left_row, count_row, pair_row = packed
        outer_prod = jnp.einsum(
            "sp,shq->hpq", left_row, right_value_grid, preferred_element_type=jnp.float32
        )
        outer_prod = outer_prod.astype(jnp.bfloat16).reshape(
            column_halfway, outer_product_width * outer_product_width
        )
        values = (
            jnp.dot(outer_prod, outer_output_weight, preferred_element_type=jnp.float32)
            + outer_output_bias
        )
        return (
            pair_row.astype(jnp.float32) + values / jnp.maximum(count_row, 1.0)[:, None]
        ).astype(jnp.bfloat16)

    current = lax.map(opm_row, (left_row_block, counts, pair_activation))
    seq_float = sequence_mask.astype(jnp.float32)
    row_mask = lax.dynamic_slice_in_dim(
        seq_float, dap_index * alignment_row_count, alignment_row_count
    )
    col_mask = lax.dynamic_slice_in_dim(seq_float, sub_index * column_halfway, column_halfway)
    pair_mask = row_mask[:, None] * col_mask[None, :]
    for which in range(2):
        current = triangle(
            current,
            pair_mask,
            pair_norm_gains[2 * which],
            pair_norm_gains[2 * which + 1],
            triangle_input_weights[which],
            triangle_output_weights[which],
            which == 0,
        )
    return current


F32, BF16 = jnp.float32, jnp.bfloat16
MESH = pl.DeviceIdType.MESH
LANES = 128


def dot(a, b, da, db):
    return lax.dot_general(a, b, (((da,), (db,)), ((), ())), preferred_element_type=F32)


def exchange(n, me, source, arrived, send_sem, recv_sem):
    def start(offset, carry):
        peer = lax.rem(me + offset, n)
        pltpu.make_async_remote_copy(
            src_ref=source(peer),
            dst_ref=arrived.at[me],
            send_sem=send_sem,
            recv_sem=recv_sem,
            device_id={"dap": peer},
            device_id_type=MESH,
        ).start()
        return carry

    lax.fori_loop(1, n, start, 0)


def await_bytes(n, arrived, sem):
    others = arrived.at[pl.ds(0, n - 1)]
    pltpu.make_async_copy(others, others, sem).wait()


def fused_kernel(
    n,
    rows,
    depth,
    x_ref,
    mask_ref,
    pair_ref,
    seq_ref,
    scale_ref,
    map_ref,
    outer_ref,
    bias_ref,
    gains_ref,
    w_in_ref,
    w_out_ref,
    out_ref,
    recv_a,
    send_b,
    recv_b,
    send_c,
    recv_c,
    wide,
    first,
    second,
    mixed_rows,
    factors,
    w_turned,
    sems,
    gather_sems,
):
    me = lax.axis_index("dap")
    barrier = pltpu.get_barrier_semaphore()

    far, chip, core = me // 8, lax.rem(me // 2, 4), lax.rem(me, 2)
    far_peers = [lax.rem(me + 8 * p, n) for p in range(1, 4)]
    chip_peers = [far * 8 + lax.rem(chip + p, 4) * 2 + core for p in range(1, 4)]
    core_peers = [me + 1 - 2 * core]
    stages = (
        (far_peers, core * 16 + chip * 4 + far, 1),
        (chip_peers, core * 16 + chip * 4, 4),
        (core_peers, core * 16, 16),
    )
    for peer in far_peers + chip_peers + core_peers:
        pl.semaphore_signal(barrier, inc=1, device_id={"dap": peer}, device_id_type=MESH)

    def forward(stage):
        peers, slot, count = stages[stage]
        held = recv_a.at[pl.ds(slot, count)]
        for peer in peers:
            pltpu.make_async_remote_copy(
                src_ref=held,
                dst_ref=held,
                send_sem=gather_sems.at[0, stage],
                recv_sem=gather_sems.at[1, stage],
                device_id={"dap": peer},
                device_id_type=MESH,
            ).start()

    def gathered(stage, way):
        blocks_moved = recv_a.at[pl.ds(0, len(stages[stage][0]) * stages[stage][2])]
        pltpu.make_async_copy(blocks_moved, blocks_moved, gather_sems.at[way, stage]).wait()

    width = pair_ref.shape[2]
    tensor = map_ref.shape[0] // 2
    per = width // n
    strip = rows * per
    blocks = tensor * depth // LANES
    high = tensor // blocks

    normed = apply_layer_norm(x_ref[...].astype(F32), scale_ref[...], 1).astype(BF16)
    mask = jnp.concatenate([mask_ref[...].astype(F32), jnp.zeros((rows, LANES - depth), F32)], axis=1)
    mask = jnp.concatenate([mask, jnp.zeros((LANES - rows, LANES), F32)], axis=0).T
    mask_col = jnp.concatenate([mask[:depth, j : j + 1] for j in range(rows)], axis=0)
    proj = dot(normed, map_ref[...], 1, 1) * mask_col
    left = proj[:, :tensor].astype(BF16)
    turned = jnp.concatenate(
        [proj, jnp.broadcast_to(mask_col, (rows * depth, LANES - 2 * tensor))], axis=1
    ).T
    pieces = []
    for j in range(rows):
        lanes = slice(j * depth, (j + 1) * depth)
        pieces.append(
            jnp.concatenate(
                [
                    turned[tensor + h * blocks : tensor + (h + 1) * blocks, lanes]
                    for h in range(high)
                ],
                axis=1,
            )
        )
    row_of = lax.broadcasted_iota(jnp.int32, (4 * rows, depth), 0) // 4
    mask_rows = jnp.zeros((4 * rows, depth), F32)
    for j in range(rows):
        spread = turned[2 * tensor : 2 * tensor + 4 * rows, j * depth : (j + 1) * depth]
        mask_rows = jnp.where(row_of == j, spread, mask_rows)
    mask_rows = jnp.concatenate([mask_rows, jnp.zeros((4 * rows, LANES - depth), F32)], axis=1)
    packed = jnp.concatenate(pieces + [mask_rows], axis=0).astype(BF16)
    recv_a[stages[0][1]] = packed
    pl.semaphore_wait(barrier, 7)
    forward(0)

    for t in range(2):
        w_turned[t] = w_in_ref[t, :, : 4 * width].astype(F32).T.astype(BF16)
    gathered(0, 1)
    forward(1)
    wide[...] = outer_ref[...].astype(F32)
    for q in range(tensor):
        weight = wide[pl.ds(q, tensor, stride=tensor), :].astype(BF16)
        factor = dot(left, weight, 1, 0).astype(BF16)
        place = (q % blocks) * LANES + (q // blocks) * depth
        for i in range(rows):
            factors[place : place + depth, i * width : (i + 1) * width] = factor[
                i * depth : (i + 1) * depth
            ]
    gathered(1, 1)
    forward(2)
    seq = seq_ref[...].astype(F32)
    lane = lax.broadcasted_iota(jnp.int32, seq.shape, 1)
    pair_mask = jnp.concatenate(
        [
            seq * jnp.sum(jnp.where(lane == me * rows + r, seq, 0.0), 1, keepdims=True)
            for r in range(rows)
        ],
        axis=1,
    )

    gathered(2, 1)
    total = n * rows
    kept = rows * blocks
    for d in range(n):
        slot = d % 2 * 16 + d // 2 % 4 * 4 + d // 8
        wide[d * kept : (d + 1) * kept, :] = recv_a[slot, :kept, :].astype(F32)
        first[d * 4 * rows : (d + 1) * 4 * rows, :] = recv_a[slot, kept:, :].astype(F32)
    right = jnp.concatenate(
        [wide[pl.ds(b, total, stride=blocks), :].astype(BF16) for b in range(blocks)], axis=1
    )
    mask_all = first[pl.ds(0, total, stride=4), :][:, :depth].astype(BF16)
    values = dot(right, factors[...], 1, 0)
    current = []
    for i in range(rows):
        own = jnp.broadcast_to(mask_col[i * depth : (i + 1) * depth], (depth, width)).astype(BF16)
        counts = dot(mask_all, own, 1, 0)
        update = (values[:, i * width : (i + 1) * width] + bias_ref[...]) / jnp.maximum(counts, 1.0)
        current.append((pair_ref[i].astype(F32) + update).astype(BF16))

    for t in range(2):
        z = jnp.concatenate([row.astype(F32) for row in current], axis=0)
        normed = apply_layer_norm(z, gains_ref[2 * t : 2 * t + 1, :], 1).astype(BF16)
        turned = dot(w_turned[t], normed, 1, 1)
        for side, scratch in ((0, first), (1, second)):
            value = turned[side * width : (side + 1) * width]
            gate = turned[(2 + side) * width : (3 + side) * width]
            gated = pair_mask * jax.nn.sigmoid(gate) * value
            for r in range(rows):
                scratch[r * width : (r + 1) * width, :] = gated[:, r * total : (r + 1) * total]
        for d in range(n):
            send_b[t, d, :strip, :] = first[pl.ds(d, strip, stride=n), :].astype(BF16)
            send_b[t, d, strip:, :] = second[pl.ds(d, strip, stride=n), :].astype(BF16)
        s = 2 + 4 * t
        exchange(n, me, lambda peer: send_b.at[t, peer], recv_b.at[t], sems.at[s], sems.at[s + 1])
        recv_b[t, me] = send_b[t, me]
        gating = jax.nn.sigmoid(dot(normed, w_in_ref[t, :, 4 * width :], 1, 0))
        gain = jnp.broadcast_to(gains_ref[2 * t + 1 : 2 * t + 2, :], (total, width)).T
        await_bytes(n, recv_b.at[t], sems.at[s + 1])
        first[...] = recv_b[t, :, :strip, :].astype(F32).reshape(n * strip, LANES)
        second[...] = recv_b[t, :, strip:, :].astype(F32).reshape(n * strip, LANES)
        for c in range(per):
            one = first[pl.ds(c, total, stride=per), :].astype(BF16)
            two = second[pl.ds(c, total, stride=per), :].astype(BF16)
            over = 1 - t
            mixed_rows[pl.ds(c, total, stride=per), :] = dot(one, two, over, over)
        send_c[t] = mixed_rows[...].astype(BF16).reshape(n, strip, LANES)
        exchange(n, me, lambda peer: send_c.at[t, peer], recv_c.at[t], sems.at[s + 2], sems.at[s + 3])
        recv_c[t, me] = send_c[t, me]
        await_bytes(n, recv_c.at[t], sems.at[s + 3])
        first[...] = recv_c[t].astype(F32).reshape(n * strip, LANES)
        following = []
        for r in range(rows):
            mixed = jnp.concatenate(
                [first[pl.ds(r * per + c, n, stride=strip), :] for c in range(per)], axis=0
            )
            mixed_norm = apply_layer_norm(mixed, gain, 0).astype(BF16)
            update = dot(mixed_norm, w_out_ref[t], 0, 0)
            block = slice(r * total, (r + 1) * total)
            following.append((z[block] + gating[block] * update).astype(BF16))
        current = following
    for r in range(rows):
        out_ref[r] = current[r]
    for stage in range(3):
        gathered(stage, 0)
    for t in range(2):
        await_bytes(n, recv_b.at[t], sems.at[2 + 4 * t])
        await_bytes(n, recv_c.at[t], sems.at[4 + 4 * t])


def fused(
    n,
    homolog_embedding,
    alignment_mask,
    pair_activation,
    sequence_mask,
    homolog_scaling_factor,
    homolog_mapping_matrix,
    outer_output_weight,
    outer_output_bias,
    pair_norm_gains,
    triangle_input_weights,
    triangle_output_weights,
):
    depth, rows, channels = homolog_embedding.shape
    total, width = pair_activation.shape[1:]
    strip = rows * (width // n)
    outer = outer_output_weight.shape[0]
    kept = rows * (homolog_mapping_matrix.shape[1] // 2) * depth // LANES
    vmem = pl.BlockSpec(memory_space=pltpu.VMEM)
    return pl.pallas_call(
        functools.partial(fused_kernel, n, rows, depth),
        out_shape=jax.ShapeDtypeStruct(pair_activation.shape, BF16),
        in_specs=[vmem] * 11,
        out_specs=vmem,
        scratch_shapes=[
            pltpu.VMEM((n, kept + 4 * rows, LANES), BF16),
            pltpu.VMEM((2, n, 2 * strip, total), BF16),
            pltpu.VMEM((2, n, 2 * strip, total), BF16),
            pltpu.VMEM((2, n, strip, total), BF16),
            pltpu.VMEM((2, n, strip, total), BF16),
            pltpu.VMEM((outer, width), F32),
            pltpu.VMEM((rows * width, LANES), F32),
            pltpu.VMEM((rows * width, LANES), F32),
            pltpu.VMEM((rows * width, LANES), F32),
            pltpu.VMEM((outer, rows * width), BF16),
            pltpu.VMEM((2, 4 * width, width), BF16),
            pltpu.SemaphoreType.DMA((10,)),
            pltpu.SemaphoreType.DMA((2, 3)),
        ],
        compiler_params=pltpu.CompilerParams(
            collective_id=0, has_side_effects=True, vmem_limit_bytes=40 * 1024 * 1024
        ),
    )(
        jnp.transpose(homolog_embedding, (1, 0, 2)).reshape(rows * depth, channels),
        jnp.transpose(alignment_mask),
        pair_activation,
        sequence_mask.reshape(1, total),
        homolog_scaling_factor.reshape(1, channels),
        jnp.transpose(homolog_mapping_matrix),
        outer_output_weight,
        outer_output_bias.reshape(1, width),
        pair_norm_gains,
        triangle_input_weights,
        triangle_output_weights,
    )


def solution(mesh):
    n, sub = mesh.shape["dap"], mesh.shape["sub"]

    def chosen(*arrays):
        depth, rows, _ = arrays[0].shape
        total, width = arrays[2].shape[1:]
        tensor = arrays[5].shape[1] // 2
        fits = (
            sub == 1
            and (depth, rows, total, width, tensor) == (32, 4, LANES, LANES, 32)
            and n * rows == total
        )
        return fused(n, *arrays) if fits else local(*arrays)
    return jax.shard_map(
        chosen,
        mesh=mesh,
        in_specs=(
            P(("grp", "sub"), "dap", None),
            P(("grp", "sub"), "dap"),
            P(("grp", "dap"), "sub", None),
            P("grp"),
            P(),
            P(),
            P(),
            P(),
            P(),
            P(),
            P(),
        ),
        out_specs=P(("grp", "dap"), "sub", None),
        check_vma=False,
    )
```

```python
import functools

import jax
import jax.numpy as jnp
from jax import lax
from jax.experimental import pallas as pl
from jax.experimental.pallas import tpu as pltpu
from jax.sharding import PartitionSpec as P


def apply_layer_norm(values, norm_gain, dimension):
    center = values - jnp.mean(values, dimension, keepdims=True)
    spread = jnp.mean(center * center, dimension, keepdims=True)
    return center * lax.rsqrt(spread + 1e-05) * norm_gain


def triangle(current, pair_mask, norm_in, norm_out, weight_in, weight_out, outgoing):
    width = weight_out.shape[0]
    normed = apply_layer_norm(current.astype(jnp.float32), norm_in, 2).astype(jnp.bfloat16)
    projected_alignment = jnp.einsum(
        "rhk,kc->crh", normed, weight_in, preferred_element_type=jnp.float32
    )
    left_value = projected_alignment[:width]
    right_value = projected_alignment[width : 2 * width]
    left_gate = projected_alignment[2 * width : 3 * width]
    right_gate = projected_alignment[3 * width : 4 * width]
    gating = jax.nn.sigmoid(projected_alignment[4 * width :])
    left_side = (pair_mask[None] * jax.nn.sigmoid(left_gate) * left_value).astype(jnp.bfloat16)
    right_side = (pair_mask[None] * jax.nn.sigmoid(right_gate) * right_value).astype(jnp.bfloat16)
    both_sides = lax.all_to_all(
        jnp.stack([left_side, right_side], axis=1), "dap", split_axis=0, concat_axis=2, tiled=True
    )
    left_channels, right_channels = both_sides[:, 0], both_sides[:, 1]
    if outgoing:
        left_full = lax.all_gather(left_channels, "sub", axis=2, tiled=True)
        right_rows = lax.all_to_all(right_channels, "sub", split_axis=1, concat_axis=2, tiled=True)
        mixed = jnp.einsum(
            "cik,cjk->cij", left_full, right_rows, preferred_element_type=jnp.float32
        )
    else:
        left_full = lax.all_gather(left_channels, "sub", axis=2, tiled=True)
        mixed = jnp.einsum(
            "cki,ckj->cij", left_full, right_channels, preferred_element_type=jnp.float32
        )
    returned = lax.all_to_all(
        mixed.astype(jnp.bfloat16), "dap", split_axis=1, concat_axis=0, tiled=True
    )
    mixed_norm = apply_layer_norm(returned.astype(jnp.float32), norm_out[:, None, None], 0).astype(
        jnp.bfloat16
    )
    update = jnp.einsum("crh,cd->drh", mixed_norm, weight_out, preferred_element_type=jnp.float32)
    return (current.astype(jnp.float32) + jnp.transpose(gating * update, (1, 2, 0))).astype(
        jnp.bfloat16
    )


def local(
    homolog_embedding,
    alignment_mask,
    pair_activation,
    sequence_mask,
    homolog_scaling_factor,
    homolog_mapping_matrix,
    outer_output_weight,
    outer_output_bias,
    pair_norm_gains,
    triangle_input_weights,
    triangle_output_weights,
):
    outer_product_width = homolog_mapping_matrix.shape[1] // 2
    alignment_row_count = pair_activation.shape[0]
    column_halfway = pair_activation.shape[1]
    row_halfway = homolog_embedding.shape[0]
    dap_index = lax.axis_index("dap")
    sub_index = lax.axis_index("sub")
    alignment_normed = apply_layer_norm(
        homolog_embedding.astype(jnp.float32), homolog_scaling_factor, 2
    ).astype(jnp.bfloat16)
    mask_as_float = alignment_mask.astype(jnp.float32)
    projected_alignment = (
        jnp.einsum(
            "ftv,vy->fty",
            alignment_normed,
            homolog_mapping_matrix,
            preferred_element_type=jnp.float32,
        )
        * mask_as_float[:, :, None]
    )
    left_proj = (
        projected_alignment[:, :, :outer_product_width]
        .astype(jnp.bfloat16)
        .reshape(row_halfway, alignment_row_count * outer_product_width)
    )
    right_proj = (
        projected_alignment[:, :, outer_product_width:]
        .astype(jnp.bfloat16)
        .reshape(row_halfway, alignment_row_count * outer_product_width)
    )
    mask_bits = mask_as_float.astype(jnp.bfloat16)
    left_complete, right_all, mask_all = (
        lax.all_gather(left_proj, "sub", axis=0, tiled=True),
        lax.all_gather(right_proj, "sub", axis=0, tiled=True),
        lax.all_gather(mask_bits, "sub", axis=0, tiled=True),
    )
    packed = jnp.concatenate([right_all, mask_all], axis=1)
    copies = jnp.broadcast_to(packed[None], (lax.axis_size("dap"),) + packed.shape)
    arrived = lax.all_to_all(copies, "dap", split_axis=0, concat_axis=0, tiled=True)
    arrived = jnp.transpose(arrived, (1, 0, 2))
    right_columns = right_all.shape[1]
    right_wide = arrived[:, :, :right_columns].reshape(arrived.shape[0], -1)
    mask_wide = arrived[:, :, right_columns:].reshape(arrived.shape[0], -1)
    right_column_block = lax.dynamic_slice_in_dim(
        right_wide,
        sub_index * (column_halfway * outer_product_width),
        column_halfway * outer_product_width,
        1,
    )
    mask_cols = lax.dynamic_slice_in_dim(mask_wide, sub_index * column_halfway, column_halfway, 1)
    alignment_mask_total = left_complete.shape[0]
    left_row_block = jnp.transpose(
        left_complete.reshape(alignment_mask_total, alignment_row_count, outer_product_width),
        (1, 0, 2),
    )
    right_value_grid = right_column_block.reshape(
        alignment_mask_total, column_halfway, outer_product_width
    )
    counts = jnp.dot(mask_all.T, mask_cols, preferred_element_type=jnp.float32)

    def opm_row(packed):
        left_row, count_row, pair_row = packed
        outer_prod = jnp.einsum(
            "sp,shq->hpq", left_row, right_value_grid, preferred_element_type=jnp.float32
        )
        outer_prod = outer_prod.astype(jnp.bfloat16).reshape(
            column_halfway, outer_product_width * outer_product_width
        )
        values = (
            jnp.dot(outer_prod, outer_output_weight, preferred_element_type=jnp.float32)
            + outer_output_bias
        )
        return (
            pair_row.astype(jnp.float32) + values / jnp.maximum(count_row, 1.0)[:, None]
        ).astype(jnp.bfloat16)

    current = lax.map(opm_row, (left_row_block, counts, pair_activation))
    seq_float = sequence_mask.astype(jnp.float32)
    row_mask = lax.dynamic_slice_in_dim(
        seq_float, dap_index * alignment_row_count, alignment_row_count
    )
    col_mask = lax.dynamic_slice_in_dim(seq_float, sub_index * column_halfway, column_halfway)
    pair_mask = row_mask[:, None] * col_mask[None, :]
    for which in range(2):
        current = triangle(
            current,
            pair_mask,
            pair_norm_gains[2 * which],
            pair_norm_gains[2 * which + 1],
            triangle_input_weights[which],
            triangle_output_weights[which],
            which == 0,
        )
    return current


F32, BF16 = jnp.float32, jnp.bfloat16
MESH = pl.DeviceIdType.MESH
LANES = 128


def dot(a, b, da, db):
    return lax.dot_general(a, b, (((da,), (db,)), ((), ())), preferred_element_type=F32)


def exchange(n, me, source, arrived, send_sem, recv_sem):
    def start(offset, carry):
        peer = lax.rem(me + offset, n)
        pltpu.make_async_remote_copy(
            src_ref=source(peer),
            dst_ref=arrived.at[me],
            send_sem=send_sem,
            recv_sem=recv_sem,
            device_id={"dap": peer},
            device_id_type=MESH,
        ).start()
        return carry

    lax.fori_loop(1, n, start, 0, unroll=True)


def await_bytes(n, arrived, sem):
    others = arrived.at[pl.ds(0, n - 1)]
    pltpu.make_async_copy(others, others, sem).wait()


def fused_kernel(
    n,
    rows,
    depth,
    x_ref,
    mask_ref,
    pair_hbm,
    seq_ref,
    scale_ref,
    map_hbm,
    outer_hbm,
    bias_ref,
    gains_ref,
    w_in_hbm,
    w_out_hbm,
    out_ref,
    recv_a,
    send_b,
    recv_b,
    send_c,
    recv_c,
    wide,
    first,
    second,
    mixed_rows,
    factors,
    w_turned,
    sems,
    gather_sems,
    map_ref,
    outer_ref,
    w_in_ref,
    pair_ref,
    w_out_ref,
    load_sems,
):
    loads = [
        pltpu.make_async_copy(far_away, near, load_sems.at[k])
        for k, (far_away, near) in enumerate(
            (
                (map_hbm, map_ref),
                (w_in_hbm, w_in_ref),
                (outer_hbm, outer_ref),
                (pair_hbm, pair_ref),
                (w_out_hbm, w_out_ref),
            )
        )
    ]
    for load in loads:
        load.start()
    me = lax.axis_index("dap")
    barrier = pltpu.get_barrier_semaphore()

    far, chip, core = me // 8, lax.rem(me // 2, 4), lax.rem(me, 2)
    far_peers = [lax.rem(me + 8 * p, n) for p in range(1, 4)]
    chip_peers = [far * 8 + lax.rem(chip + p, 4) * 2 + core for p in range(1, 4)]
    core_peers = [me + 1 - 2 * core]
    stages = (
        (far_peers, core * 16 + chip * 4 + far, 1),
        (chip_peers, core * 16 + chip * 4, 4),
        (core_peers, core * 16, 16),
    )
    for peer in far_peers + chip_peers + core_peers:
        pl.semaphore_signal(barrier, inc=1, device_id={"dap": peer}, device_id_type=MESH)

    def forward(stage):
        peers, slot, count = stages[stage]
        held = recv_a.at[pl.ds(slot, count)]
        for peer in peers:
            pltpu.make_async_remote_copy(
                src_ref=held,
                dst_ref=held,
                send_sem=gather_sems.at[0, stage],
                recv_sem=gather_sems.at[1, stage],
                device_id={"dap": peer},
                device_id_type=MESH,
            ).start()

    def gathered(stage, way):
        blocks_moved = recv_a.at[pl.ds(0, len(stages[stage][0]) * stages[stage][2])]
        pltpu.make_async_copy(blocks_moved, blocks_moved, gather_sems.at[way, stage]).wait()

    width = pair_ref.shape[2]
    tensor = map_ref.shape[0] // 2
    per = width // n
    strip = rows * per
    blocks = tensor * depth // LANES
    high = tensor // blocks

    normed = apply_layer_norm(x_ref[...].astype(F32), scale_ref[...], 1).astype(BF16)
    mask = jnp.concatenate([mask_ref[...].astype(F32), jnp.zeros((rows, LANES - depth), F32)], axis=1)
    mask = jnp.concatenate([mask, jnp.zeros((LANES - rows, LANES), F32)], axis=0).T
    mask_col = jnp.concatenate([mask[:depth, j : j + 1] for j in range(rows)], axis=0)
    loads[0].wait()
    proj = dot(normed, map_ref[...], 1, 1) * mask_col
    left = proj[:, :tensor].astype(BF16)
    turned = jnp.concatenate(
        [proj, jnp.broadcast_to(mask_col, (rows * depth, LANES - 2 * tensor))], axis=1
    ).T
    pieces = []
    for j in range(rows):
        lanes = slice(j * depth, (j + 1) * depth)
        pieces.append(
            jnp.concatenate(
                [
                    turned[tensor + h * blocks : tensor + (h + 1) * blocks, lanes]
                    for h in range(high)
                ],
                axis=1,
            )
        )
    row_of = lax.broadcasted_iota(jnp.int32, (4 * rows, depth), 0) // 4
    mask_rows = jnp.zeros((4 * rows, depth), F32)
    for j in range(rows):
        spread = turned[2 * tensor : 2 * tensor + 4 * rows, j * depth : (j + 1) * depth]
        mask_rows = jnp.where(row_of == j, spread, mask_rows)
    mask_rows = jnp.concatenate([mask_rows, jnp.zeros((4 * rows, LANES - depth), F32)], axis=1)
    packed = jnp.concatenate(pieces + [mask_rows], axis=0).astype(BF16)
    recv_a[stages[0][1]] = packed
    pl.semaphore_wait(barrier, 7)
    forward(0)

    loads[1].wait()
    for t in range(2):
        w_turned[t] = w_in_ref[t, :, : 4 * width].astype(F32).T.astype(BF16)
    gathered(0, 1)
    forward(1)
    loads[2].wait()
    wide[...] = outer_ref[...].astype(F32)
    for q in range(tensor):
        weight = wide[pl.ds(q, tensor, stride=tensor), :].astype(BF16)
        factor = dot(left, weight, 1, 0).astype(BF16)
        place = (q % blocks) * LANES + (q // blocks) * depth
        for i in range(rows):
            factors[place : place + depth, i * width : (i + 1) * width] = factor[
                i * depth : (i + 1) * depth
            ]
    gathered(1, 1)
    forward(2)
    loads[3].wait()
    loads[4].wait()
    seq = seq_ref[...].astype(F32)
    lane = lax.broadcasted_iota(jnp.int32, seq.shape, 1)
    pair_mask = jnp.concatenate(
        [
            seq * jnp.sum(jnp.where(lane == me * rows + r, seq, 0.0), 1, keepdims=True)
            for r in range(rows)
        ],
        axis=1,
    )

    gathered(2, 1)
    total = n * rows
    kept = rows * blocks
    for d in range(n):
        slot = d % 2 * 16 + d // 2 % 4 * 4 + d // 8
        wide[d * kept : (d + 1) * kept, :] = recv_a[slot, :kept, :].astype(F32)
        first[d * 4 * rows : (d + 1) * 4 * rows, :] = recv_a[slot, kept:, :].astype(F32)
    right = jnp.concatenate(
        [wide[pl.ds(b, total, stride=blocks), :].astype(BF16) for b in range(blocks)], axis=1
    )
    mask_all = first[pl.ds(0, total, stride=4), :][:, :depth].astype(BF16)
    values = dot(right, factors[...], 1, 0)
    current = []
    for i in range(rows):
        own = jnp.broadcast_to(mask_col[i * depth : (i + 1) * depth], (depth, width)).astype(BF16)
        counts = dot(mask_all, own, 1, 0)
        update = (values[:, i * width : (i + 1) * width] + bias_ref[...]) / jnp.maximum(counts, 1.0)
        current.append((pair_ref[i].astype(F32) + update).astype(BF16))

    for t in range(2):
        z = jnp.concatenate([row.astype(F32) for row in current], axis=0)
        normed = apply_layer_norm(z, gains_ref[2 * t : 2 * t + 1, :], 1).astype(BF16)
        turned = dot(w_turned[t], normed, 1, 1)
        for side, scratch in ((0, first), (1, second)):
            value = turned[side * width : (side + 1) * width]
            gate = turned[(2 + side) * width : (3 + side) * width]
            gated = pair_mask * jax.nn.sigmoid(gate) * value
            for r in range(rows):
                scratch[r * width : (r + 1) * width, :] = gated[:, r * total : (r + 1) * total]
            for d in range(n):
                send_b[t, side, d] = scratch[pl.ds(d, strip, stride=n), :].astype(BF16)
            exchange(
                n,
                me,
                lambda peer: send_b.at[t, side, peer],
                recv_b.at[t, side],
                sems.at[t, side, 0],
                sems.at[t, side, 1],
            )
            recv_b[t, side, me] = send_b[t, side, me]
        gating = jax.nn.sigmoid(dot(normed, w_in_ref[t, :, 4 * width :], 1, 0))
        gain = jnp.broadcast_to(gains_ref[2 * t + 1 : 2 * t + 2, :], (total, width)).T
        for side, scratch in ((0, first), (1, second)):
            await_bytes(n, recv_b.at[t, side], sems.at[t, side, 1])
            scratch[...] = recv_b[t, side].astype(F32).reshape(n * strip, LANES)
        for c in range(per):
            one = first[pl.ds(c, total, stride=per), :].astype(BF16)
            two = second[pl.ds(c, total, stride=per), :].astype(BF16)
            over = 1 - t
            mixed_rows[pl.ds(c, total, stride=per), :] = dot(one, two, over, over)
        send_c[t] = mixed_rows[...].astype(BF16).reshape(n, strip, LANES)
        exchange(n, me, lambda peer: send_c.at[t, peer], recv_c.at[t], sems.at[t, 2, 0], sems.at[t, 2, 1])
        recv_c[t, me] = send_c[t, me]
        await_bytes(n, recv_c.at[t], sems.at[t, 2, 1])
        first[...] = recv_c[t].astype(F32).reshape(n * strip, LANES)
        following = []
        for r in range(rows):
            mixed = jnp.concatenate(
                [first[pl.ds(r * per + c, n, stride=strip), :] for c in range(per)], axis=0
            )
            mixed_norm = apply_layer_norm(mixed, gain, 0).astype(BF16)
            update = dot(mixed_norm, w_out_ref[t], 0, 0)
            block = slice(r * total, (r + 1) * total)
            following.append((z[block] + gating[block] * update).astype(BF16))
        current = following
    for r in range(rows):
        out_ref[r] = current[r]
    for stage in range(3):
        gathered(stage, 0)
    for t in range(2):
        for side in range(2):
            await_bytes(n, recv_b.at[t, side], sems.at[t, side, 0])
        await_bytes(n, recv_c.at[t], sems.at[t, 2, 0])


def fused(
    n,
    homolog_embedding,
    alignment_mask,
    pair_activation,
    sequence_mask,
    homolog_scaling_factor,
    homolog_mapping_matrix,
    outer_output_weight,
    outer_output_bias,
    pair_norm_gains,
    triangle_input_weights,
    triangle_output_weights,
):
    depth, rows, channels = homolog_embedding.shape
    total, width = pair_activation.shape[1:]
    strip = rows * (width // n)
    outer = outer_output_weight.shape[0]
    kept = rows * (homolog_mapping_matrix.shape[1] // 2) * depth // LANES
    vmem = pl.BlockSpec(memory_space=pltpu.VMEM)
    hbm = pl.BlockSpec(memory_space=pltpu.HBM)
    return pl.pallas_call(
        functools.partial(fused_kernel, n, rows, depth),
        out_shape=jax.ShapeDtypeStruct(pair_activation.shape, BF16),
        in_specs=[vmem, vmem, hbm, vmem, vmem, hbm, hbm, vmem, vmem, hbm, hbm],
        out_specs=vmem,
        scratch_shapes=[
            pltpu.VMEM((n, kept + 4 * rows, LANES), BF16),
            pltpu.VMEM((2, 2, n, strip, total), BF16),
            pltpu.VMEM((2, 2, n, strip, total), BF16),
            pltpu.VMEM((2, n, strip, total), BF16),
            pltpu.VMEM((2, n, strip, total), BF16),
            pltpu.VMEM((outer, width), F32),
            pltpu.VMEM((rows * width, LANES), F32),
            pltpu.VMEM((rows * width, LANES), F32),
            pltpu.VMEM((rows * width, LANES), F32),
            pltpu.VMEM((outer, rows * width), BF16),
            pltpu.VMEM((2, 4 * width, width), BF16),
            pltpu.SemaphoreType.DMA((2, 3, 2)),
            pltpu.SemaphoreType.DMA((2, 3)),
            pltpu.VMEM(homolog_mapping_matrix.shape[::-1], BF16),
            pltpu.VMEM(outer_output_weight.shape, BF16),
            pltpu.VMEM(triangle_input_weights.shape, BF16),
            pltpu.VMEM(pair_activation.shape, BF16),
            pltpu.VMEM(triangle_output_weights.shape, BF16),
            pltpu.SemaphoreType.DMA((5,)),
        ],
        compiler_params=pltpu.CompilerParams(
            collective_id=0, has_side_effects=True, vmem_limit_bytes=62 * 1024 * 1024
        ),
    )(
        jnp.transpose(homolog_embedding, (1, 0, 2)).reshape(rows * depth, channels),
        jnp.transpose(alignment_mask),
        pair_activation,
        sequence_mask.reshape(1, total),
        homolog_scaling_factor.reshape(1, channels),
        jnp.transpose(homolog_mapping_matrix),
        outer_output_weight,
        outer_output_bias.reshape(1, width),
        pair_norm_gains,
        triangle_input_weights,
        triangle_output_weights,
    )


def solution(mesh):
    n, sub = mesh.shape["dap"], mesh.shape["sub"]

    def chosen(*arrays):
        depth, rows, _ = arrays[0].shape
        total, width = arrays[2].shape[1:]
        tensor = arrays[5].shape[1] // 2
        fits = (
            sub == 1
            and (depth, rows, total, width, tensor) == (32, 4, LANES, LANES, 32)
            and n * rows == total
        )
        return fused(n, *arrays) if fits else local(*arrays)
    return jax.shard_map(
        chosen,
        mesh=mesh,
        in_specs=(
            P(("grp", "sub"), "dap", None),
            P(("grp", "sub"), "dap"),
            P(("grp", "dap"), "sub", None),
            P("grp"),
            P(),
            P(),
            P(),
            P(),
            P(),
            P(),
            P(),
        ),
        out_specs=P(("grp", "dap"), "sub", None),
        check_vma=False,
    )
```

```python
import functools

import jax
import jax.numpy as jnp
from jax import lax
from jax.experimental import pallas as pl
from jax.experimental.pallas import tpu as pltpu
from jax.sharding import PartitionSpec as P


def apply_layer_norm(values, norm_gain, dimension):
    center = values - jnp.mean(values, dimension, keepdims=True)
    spread = jnp.mean(center * center, dimension, keepdims=True)
    return center * lax.rsqrt(spread + 1e-05) * norm_gain


def triangle(current, pair_mask, norm_in, norm_out, weight_in, weight_out, outgoing):
    width = weight_out.shape[0]
    normed = apply_layer_norm(current.astype(jnp.float32), norm_in, 2).astype(jnp.bfloat16)
    projected_alignment = jnp.einsum(
        "rhk,kc->crh", normed, weight_in, preferred_element_type=jnp.float32
    )
    left_value = projected_alignment[:width]
    right_value = projected_alignment[width : 2 * width]
    left_gate = projected_alignment[2 * width : 3 * width]
    right_gate = projected_alignment[3 * width : 4 * width]
    gating = jax.nn.sigmoid(projected_alignment[4 * width :])
    left_side = (pair_mask[None] * jax.nn.sigmoid(left_gate) * left_value).astype(jnp.bfloat16)
    right_side = (pair_mask[None] * jax.nn.sigmoid(right_gate) * right_value).astype(jnp.bfloat16)
    both_sides = lax.all_to_all(
        jnp.stack([left_side, right_side], axis=1), "dap", split_axis=0, concat_axis=2, tiled=True
    )
    left_channels, right_channels = both_sides[:, 0], both_sides[:, 1]
    if outgoing:
        left_full = lax.all_gather(left_channels, "sub", axis=2, tiled=True)
        right_rows = lax.all_to_all(right_channels, "sub", split_axis=1, concat_axis=2, tiled=True)
        mixed = jnp.einsum(
            "cik,cjk->cij", left_full, right_rows, preferred_element_type=jnp.float32
        )
    else:
        left_full = lax.all_gather(left_channels, "sub", axis=2, tiled=True)
        mixed = jnp.einsum(
            "cki,ckj->cij", left_full, right_channels, preferred_element_type=jnp.float32
        )
    returned = lax.all_to_all(
        mixed.astype(jnp.bfloat16), "dap", split_axis=1, concat_axis=0, tiled=True
    )
    mixed_norm = apply_layer_norm(returned.astype(jnp.float32), norm_out[:, None, None], 0).astype(
        jnp.bfloat16
    )
    update = jnp.einsum("crh,cd->drh", mixed_norm, weight_out, preferred_element_type=jnp.float32)
    return (current.astype(jnp.float32) + jnp.transpose(gating * update, (1, 2, 0))).astype(
        jnp.bfloat16
    )


def local(
    homolog_embedding,
    alignment_mask,
    pair_activation,
    sequence_mask,
    homolog_scaling_factor,
    homolog_mapping_matrix,
    outer_output_weight,
    outer_output_bias,
    pair_norm_gains,
    triangle_input_weights,
    triangle_output_weights,
):
    outer_product_width = homolog_mapping_matrix.shape[1] // 2
    alignment_row_count = pair_activation.shape[0]
    column_halfway = pair_activation.shape[1]
    row_halfway = homolog_embedding.shape[0]
    dap_index = lax.axis_index("dap")
    sub_index = lax.axis_index("sub")
    alignment_normed = apply_layer_norm(
        homolog_embedding.astype(jnp.float32), homolog_scaling_factor, 2
    ).astype(jnp.bfloat16)
    mask_as_float = alignment_mask.astype(jnp.float32)
    projected_alignment = (
        jnp.einsum(
            "ftv,vy->fty",
            alignment_normed,
            homolog_mapping_matrix,
            preferred_element_type=jnp.float32,
        )
        * mask_as_float[:, :, None]
    )
    left_proj = (
        projected_alignment[:, :, :outer_product_width]
        .astype(jnp.bfloat16)
        .reshape(row_halfway, alignment_row_count * outer_product_width)
    )
    right_proj = (
        projected_alignment[:, :, outer_product_width:]
        .astype(jnp.bfloat16)
        .reshape(row_halfway, alignment_row_count * outer_product_width)
    )
    mask_bits = mask_as_float.astype(jnp.bfloat16)
    left_complete, right_all, mask_all = (
        lax.all_gather(left_proj, "sub", axis=0, tiled=True),
        lax.all_gather(right_proj, "sub", axis=0, tiled=True),
        lax.all_gather(mask_bits, "sub", axis=0, tiled=True),
    )
    packed = jnp.concatenate([right_all, mask_all], axis=1)
    copies = jnp.broadcast_to(packed[None], (lax.axis_size("dap"),) + packed.shape)
    arrived = lax.all_to_all(copies, "dap", split_axis=0, concat_axis=0, tiled=True)
    arrived = jnp.transpose(arrived, (1, 0, 2))
    right_columns = right_all.shape[1]
    right_wide = arrived[:, :, :right_columns].reshape(arrived.shape[0], -1)
    mask_wide = arrived[:, :, right_columns:].reshape(arrived.shape[0], -1)
    right_column_block = lax.dynamic_slice_in_dim(
        right_wide,
        sub_index * (column_halfway * outer_product_width),
        column_halfway * outer_product_width,
        1,
    )
    mask_cols = lax.dynamic_slice_in_dim(mask_wide, sub_index * column_halfway, column_halfway, 1)
    alignment_mask_total = left_complete.shape[0]
    left_row_block = jnp.transpose(
        left_complete.reshape(alignment_mask_total, alignment_row_count, outer_product_width),
        (1, 0, 2),
    )
    right_value_grid = right_column_block.reshape(
        alignment_mask_total, column_halfway, outer_product_width
    )
    counts = jnp.dot(mask_all.T, mask_cols, preferred_element_type=jnp.float32)

    def opm_row(packed):
        left_row, count_row, pair_row = packed
        outer_prod = jnp.einsum(
            "sp,shq->hpq", left_row, right_value_grid, preferred_element_type=jnp.float32
        )
        outer_prod = outer_prod.astype(jnp.bfloat16).reshape(
            column_halfway, outer_product_width * outer_product_width
        )
        values = (
            jnp.dot(outer_prod, outer_output_weight, preferred_element_type=jnp.float32)
            + outer_output_bias
        )
        return (
            pair_row.astype(jnp.float32) + values / jnp.maximum(count_row, 1.0)[:, None]
        ).astype(jnp.bfloat16)

    current = lax.map(opm_row, (left_row_block, counts, pair_activation))
    seq_float = sequence_mask.astype(jnp.float32)
    row_mask = lax.dynamic_slice_in_dim(
        seq_float, dap_index * alignment_row_count, alignment_row_count
    )
    col_mask = lax.dynamic_slice_in_dim(seq_float, sub_index * column_halfway, column_halfway)
    pair_mask = row_mask[:, None] * col_mask[None, :]
    for which in range(2):
        current = triangle(
            current,
            pair_mask,
            pair_norm_gains[2 * which],
            pair_norm_gains[2 * which + 1],
            triangle_input_weights[which],
            triangle_output_weights[which],
            which == 0,
        )
    return current


F32, BF16 = jnp.float32, jnp.bfloat16
MESH = pl.DeviceIdType.MESH
LANES = 128


def dot(a, b, da, db):
    return lax.dot_general(a, b, (((da,), (db,)), ((), ())), preferred_element_type=F32)


def exchange(n, me, source, arrived, send_sem, recv_sem):
    def start(offset, carry):
        peer = lax.rem(me + offset, n)
        pltpu.make_async_remote_copy(
            src_ref=source(peer),
            dst_ref=arrived.at[me],
            send_sem=send_sem,
            recv_sem=recv_sem,
            device_id={"dap": peer},
            device_id_type=MESH,
        ).start()
        return carry

    lax.fori_loop(1, n, start, 0, unroll=True)


def await_bytes(n, arrived, sem):
    others = arrived.at[pl.ds(0, n - 1)]
    pltpu.make_async_copy(others, others, sem).wait()


def fused_kernel(
    n,
    rows,
    depth,
    x_ref,
    mask_ref,
    pair_hbm,
    seq_ref,
    scale_ref,
    map_hbm,
    outer_hbm,
    bias_ref,
    gains_ref,
    w_in_hbm,
    w_out_hbm,
    out_ref,
    recv_a,
    send_b,
    recv_b,
    send_c,
    recv_c,
    wide,
    first,
    second,
    mixed_rows,
    factors,
    w_turned,
    sems,
    gather_sems,
    map_ref,
    outer_ref,
    w_in_ref,
    pair_ref,
    w_out_ref,
    load_sems,
):
    loads = [
        pltpu.make_async_copy(far_away, near, load_sems.at[k])
        for k, (far_away, near) in enumerate(
            (
                (map_hbm, map_ref),
                (w_in_hbm, w_in_ref),
                (outer_hbm, outer_ref),
                (pair_hbm, pair_ref),
                (w_out_hbm, w_out_ref),
            )
        )
    ]
    for load in loads:
        load.start()
    me = lax.axis_index("dap")
    barrier = pltpu.get_barrier_semaphore()

    far, chip, core = me // 8, lax.rem(me // 2, 4), lax.rem(me, 2)
    far_peers = [lax.rem(me + 8 * p, n) for p in range(1, 4)]
    chip_peers = [far * 8 + lax.rem(chip + p, 4) * 2 + core for p in range(1, 4)]
    core_peers = [me + 1 - 2 * core]
    column = core * 16 + chip * 4
    own_slot = column + far
    for peer in far_peers + chip_peers + core_peers:
        pl.semaphore_signal(barrier, inc=1, device_id={"dap": peer}, device_id_type=MESH)

    def forward(peers, slot, count, send, arrivals):
        held = recv_a.at[pl.ds(slot, count)]
        for peer, arrival in zip(peers, arrivals):
            pltpu.make_async_remote_copy(
                src_ref=held,
                dst_ref=held,
                send_sem=gather_sems.at[send],
                recv_sem=gather_sems.at[arrival],
                device_id={"dap": peer},
                device_id_type=MESH,
            ).start()

    def gathered(count, sem):
        blocks_moved = recv_a.at[pl.ds(0, count)]
        pltpu.make_async_copy(blocks_moved, blocks_moved, gather_sems.at[sem]).wait()

    width = pair_ref.shape[2]
    tensor = map_ref.shape[0] // 2
    per = width // n
    strip = rows * per
    blocks = tensor * depth // LANES
    high = tensor // blocks

    normed = apply_layer_norm(x_ref[...].astype(F32), scale_ref[...], 1).astype(BF16)
    mask = jnp.concatenate([mask_ref[...].astype(F32), jnp.zeros((rows, LANES - depth), F32)], axis=1)
    mask = jnp.concatenate([mask, jnp.zeros((LANES - rows, LANES), F32)], axis=0).T
    mask_col = jnp.concatenate([mask[:depth, j : j + 1] for j in range(rows)], axis=0)
    loads[0].wait()
    proj = dot(normed, map_ref[...], 1, 1) * mask_col
    left = proj[:, :tensor].astype(BF16)
    turned = jnp.concatenate(
        [proj, jnp.broadcast_to(mask_col, (rows * depth, LANES - 2 * tensor))], axis=1
    ).T
    pieces = []
    for j in range(rows):
        lanes = slice(j * depth, (j + 1) * depth)
        pieces.append(
            jnp.concatenate(
                [
                    turned[tensor + h * blocks : tensor + (h + 1) * blocks, lanes]
                    for h in range(high)
                ],
                axis=1,
            )
        )
    row_of = lax.broadcasted_iota(jnp.int32, (4 * rows, depth), 0) // 4
    mask_rows = jnp.zeros((4 * rows, depth), F32)
    for j in range(rows):
        spread = turned[2 * tensor : 2 * tensor + 4 * rows, j * depth : (j + 1) * depth]
        mask_rows = jnp.where(row_of == j, spread, mask_rows)
    mask_rows = jnp.concatenate([mask_rows, jnp.zeros((4 * rows, LANES - depth), F32)], axis=1)
    packed = jnp.concatenate(pieces + [mask_rows], axis=0).astype(BF16)
    recv_a[own_slot] = packed
    pl.semaphore_wait(barrier, 7)
    forward(far_peers, own_slot, 1, 0, (3, 4, 5))
    forward(chip_peers, own_slot, 1, 1, (6, 7, 8))

    for p in range(1, 4):
        gathered(1, 2 + p)
        forward(chip_peers, column + lax.rem(far + 4 - p, 4), 1, 1, (6, 7, 8))
    forward(core_peers, column, 4, 2, (9,))
    loads[2].wait()
    wide[...] = outer_ref[...].astype(F32)
    for q in range(tensor):
        weight = wide[pl.ds(q, tensor, stride=tensor), :].astype(BF16)
        factor = dot(left, weight, 1, 0).astype(BF16)
        place = (q % blocks) * LANES + (q // blocks) * depth
        for i in range(rows):
            factors[place : place + depth, i * width : (i + 1) * width] = factor[
                i * depth : (i + 1) * depth
            ]
    for p in range(1, 4):
        gathered(4, 5 + p)
        forward(core_peers, core * 16 + lax.rem(chip + 4 - p, 4) * 4, 4, 2, (9,))
    loads[1].wait()
    for t in range(2):
        w_turned[t] = w_in_ref[t, :, : 4 * width].astype(F32).T.astype(BF16)
    loads[3].wait()
    loads[4].wait()
    seq = seq_ref[...].astype(F32)
    lane = lax.broadcasted_iota(jnp.int32, seq.shape, 1)
    pair_mask = jnp.concatenate(
        [
            seq * jnp.sum(jnp.where(lane == me * rows + r, seq, 0.0), 1, keepdims=True)
            for r in range(rows)
        ],
        axis=1,
    )

    gathered(16, 9)
    total = n * rows
    kept = rows * blocks
    for d in range(n):
        slot = d % 2 * 16 + d // 2 % 4 * 4 + d // 8
        wide[d * kept : (d + 1) * kept, :] = recv_a[slot, :kept, :].astype(F32)
        first[d * 4 * rows : (d + 1) * 4 * rows, :] = recv_a[slot, kept:, :].astype(F32)
    right = jnp.concatenate(
        [wide[pl.ds(b, total, stride=blocks), :].astype(BF16) for b in range(blocks)], axis=1
    )
    mask_all = first[pl.ds(0, total, stride=4), :][:, :depth].astype(BF16)
    values = dot(right, factors[...], 1, 0)
    current = []
    for i in range(rows):
        own = jnp.broadcast_to(mask_col[i * depth : (i + 1) * depth], (depth, width)).astype(BF16)
        counts = dot(mask_all, own, 1, 0)
        update = (values[:, i * width : (i + 1) * width] + bias_ref[...]) / jnp.maximum(counts, 1.0)
        current.append((pair_ref[i].astype(F32) + update).astype(BF16))

    for t in range(2):
        z = jnp.concatenate([row.astype(F32) for row in current], axis=0)
        normed = apply_layer_norm(z, gains_ref[2 * t : 2 * t + 1, :], 1).astype(BF16)
        turned = dot(w_turned[t], normed, 1, 1)
        for side, scratch in ((0, first), (1, second)):
            value = turned[side * width : (side + 1) * width]
            gate = turned[(2 + side) * width : (3 + side) * width]
            gated = pair_mask * jax.nn.sigmoid(gate) * value
            for r in range(rows):
                scratch[r * width : (r + 1) * width, :] = gated[:, r * total : (r + 1) * total]
            for d in range(n):
                send_b[t, side, d] = scratch[pl.ds(d, strip, stride=n), :].astype(BF16)
            exchange(
                n,
                me,
                lambda peer: send_b.at[t, side, peer],
                recv_b.at[t, side],
                sems.at[t, side, 0],
                sems.at[t, side, 1],
            )
            recv_b[t, side, me] = send_b[t, side, me]
        gating = jax.nn.sigmoid(dot(normed, w_in_ref[t, :, 4 * width :], 1, 0))
        gain = jnp.broadcast_to(gains_ref[2 * t + 1 : 2 * t + 2, :], (total, width)).T
        for side, scratch in ((0, first), (1, second)):
            await_bytes(n, recv_b.at[t, side], sems.at[t, side, 1])
            scratch[...] = recv_b[t, side].astype(F32).reshape(n * strip, LANES)
        for c in range(per):
            one = first[pl.ds(c, total, stride=per), :].astype(BF16)
            two = second[pl.ds(c, total, stride=per), :].astype(BF16)
            over = 1 - t
            mixed_rows[pl.ds(c, total, stride=per), :] = dot(one, two, over, over)
        send_c[t] = mixed_rows[...].astype(BF16).reshape(n, strip, LANES)
        exchange(n, me, lambda peer: send_c.at[t, peer], recv_c.at[t], sems.at[t, 2, 0], sems.at[t, 2, 1])
        recv_c[t, me] = send_c[t, me]
        await_bytes(n, recv_c.at[t], sems.at[t, 2, 1])
        first[...] = recv_c[t].astype(F32).reshape(n * strip, LANES)
        following = []
        for r in range(rows):
            mixed = jnp.concatenate(
                [first[pl.ds(r * per + c, n, stride=strip), :] for c in range(per)], axis=0
            )
            mixed_norm = apply_layer_norm(mixed, gain, 0).astype(BF16)
            update = dot(mixed_norm, w_out_ref[t], 0, 0)
            block = slice(r * total, (r + 1) * total)
            following.append((z[block] + gating[block] * update).astype(BF16))
        current = following
    for r in range(rows):
        out_ref[r] = current[r]
    for stage, count in enumerate((3, 12, 16)):
        gathered(count, stage)
    for t in range(2):
        for side in range(2):
            await_bytes(n, recv_b.at[t, side], sems.at[t, side, 0])
        await_bytes(n, recv_c.at[t], sems.at[t, 2, 0])


def fused(
    n,
    homolog_embedding,
    alignment_mask,
    pair_activation,
    sequence_mask,
    homolog_scaling_factor,
    homolog_mapping_matrix,
    outer_output_weight,
    outer_output_bias,
    pair_norm_gains,
    triangle_input_weights,
    triangle_output_weights,
):
    depth, rows, channels = homolog_embedding.shape
    total, width = pair_activation.shape[1:]
    strip = rows * (width // n)
    outer = outer_output_weight.shape[0]
    kept = rows * (homolog_mapping_matrix.shape[1] // 2) * depth // LANES
    vmem = pl.BlockSpec(memory_space=pltpu.VMEM)
    hbm = pl.BlockSpec(memory_space=pltpu.HBM)
    return pl.pallas_call(
        functools.partial(fused_kernel, n, rows, depth),
        out_shape=jax.ShapeDtypeStruct(pair_activation.shape, BF16),
        in_specs=[vmem, vmem, hbm, vmem, vmem, hbm, hbm, vmem, vmem, hbm, hbm],
        out_specs=vmem,
        scratch_shapes=[
            pltpu.VMEM((n, kept + 4 * rows, LANES), BF16),
            pltpu.VMEM((2, 2, n, strip, total), BF16),
            pltpu.VMEM((2, 2, n, strip, total), BF16),
            pltpu.VMEM((2, n, strip, total), BF16),
            pltpu.VMEM((2, n, strip, total), BF16),
            pltpu.VMEM((outer, width), F32),
            pltpu.VMEM((rows * width, LANES), F32),
            pltpu.VMEM((rows * width, LANES), F32),
            pltpu.VMEM((rows * width, LANES), F32),
            pltpu.VMEM((outer, rows * width), BF16),
            pltpu.VMEM((2, 4 * width, width), BF16),
            pltpu.SemaphoreType.DMA((2, 3, 2)),
            pltpu.SemaphoreType.DMA((10,)),
            pltpu.VMEM(homolog_mapping_matrix.shape[::-1], BF16),
            pltpu.VMEM(outer_output_weight.shape, BF16),
            pltpu.VMEM(triangle_input_weights.shape, BF16),
            pltpu.VMEM(pair_activation.shape, BF16),
            pltpu.VMEM(triangle_output_weights.shape, BF16),
            pltpu.SemaphoreType.DMA((5,)),
        ],
        compiler_params=pltpu.CompilerParams(
            collective_id=0, has_side_effects=True, vmem_limit_bytes=62 * 1024 * 1024
        ),
    )(
        jnp.transpose(homolog_embedding, (1, 0, 2)).reshape(rows * depth, channels),
        jnp.transpose(alignment_mask),
        pair_activation,
        sequence_mask.reshape(1, total),
        homolog_scaling_factor.reshape(1, channels),
        jnp.transpose(homolog_mapping_matrix),
        outer_output_weight,
        outer_output_bias.reshape(1, width),
        pair_norm_gains,
        triangle_input_weights,
        triangle_output_weights,
    )


def solution(mesh):
    n, sub = mesh.shape["dap"], mesh.shape["sub"]

    def chosen(*arrays):
        depth, rows, _ = arrays[0].shape
        total, width = arrays[2].shape[1:]
        tensor = arrays[5].shape[1] // 2
        fits = (
            sub == 1
            and (depth, rows, total, width, tensor) == (32, 4, LANES, LANES, 32)
            and n * rows == total
        )
        return fused(n, *arrays) if fits else local(*arrays)
    return jax.shard_map(
        chosen,
        mesh=mesh,
        in_specs=(
            P(("grp", "sub"), "dap", None),
            P(("grp", "sub"), "dap"),
            P(("grp", "dap"), "sub", None),
            P("grp"),
            P(),
            P(),
            P(),
            P(),
            P(),
            P(),
            P(),
        ),
        out_specs=P(("grp", "dap"), "sub", None),
        check_vma=False,
    )
```

```python
import functools

import jax
import jax.numpy as jnp
from jax import lax
from jax.experimental import pallas as pl
from jax.experimental.pallas import tpu as pltpu
from jax.sharding import PartitionSpec as P


def apply_layer_norm(values, norm_gain, dimension):
    center = values - jnp.mean(values, dimension, keepdims=True)
    spread = jnp.mean(center * center, dimension, keepdims=True)
    return center * lax.rsqrt(spread + 1e-05) * norm_gain


def triangle(current, pair_mask, norm_in, norm_out, weight_in, weight_out, outgoing):
    width = weight_out.shape[0]
    normed = apply_layer_norm(current.astype(jnp.float32), norm_in, 2).astype(jnp.bfloat16)
    projected_alignment = jnp.einsum(
        "rhk,kc->crh", normed, weight_in, preferred_element_type=jnp.float32
    )
    left_value = projected_alignment[:width]
    right_value = projected_alignment[width : 2 * width]
    left_gate = projected_alignment[2 * width : 3 * width]
    right_gate = projected_alignment[3 * width : 4 * width]
    gating = jax.nn.sigmoid(projected_alignment[4 * width :])
    left_side = (pair_mask[None] * jax.nn.sigmoid(left_gate) * left_value).astype(jnp.bfloat16)
    right_side = (pair_mask[None] * jax.nn.sigmoid(right_gate) * right_value).astype(jnp.bfloat16)
    both_sides = lax.all_to_all(
        jnp.stack([left_side, right_side], axis=1), "dap", split_axis=0, concat_axis=2, tiled=True
    )
    left_channels, right_channels = both_sides[:, 0], both_sides[:, 1]
    if outgoing:
        left_full = lax.all_gather(left_channels, "sub", axis=2, tiled=True)
        right_rows = lax.all_to_all(right_channels, "sub", split_axis=1, concat_axis=2, tiled=True)
        mixed = jnp.einsum(
            "cik,cjk->cij", left_full, right_rows, preferred_element_type=jnp.float32
        )
    else:
        left_full = lax.all_gather(left_channels, "sub", axis=2, tiled=True)
        mixed = jnp.einsum(
            "cki,ckj->cij", left_full, right_channels, preferred_element_type=jnp.float32
        )
    returned = lax.all_to_all(
        mixed.astype(jnp.bfloat16), "dap", split_axis=1, concat_axis=0, tiled=True
    )
    mixed_norm = apply_layer_norm(returned.astype(jnp.float32), norm_out[:, None, None], 0).astype(
        jnp.bfloat16
    )
    update = jnp.einsum("crh,cd->drh", mixed_norm, weight_out, preferred_element_type=jnp.float32)
    return (current.astype(jnp.float32) + jnp.transpose(gating * update, (1, 2, 0))).astype(
        jnp.bfloat16
    )


def local(
    homolog_embedding,
    alignment_mask,
    pair_activation,
    sequence_mask,
    homolog_scaling_factor,
    homolog_mapping_matrix,
    outer_output_weight,
    outer_output_bias,
    pair_norm_gains,
    triangle_input_weights,
    triangle_output_weights,
):
    outer_product_width = homolog_mapping_matrix.shape[1] // 2
    alignment_row_count = pair_activation.shape[0]
    column_halfway = pair_activation.shape[1]
    row_halfway = homolog_embedding.shape[0]
    dap_index = lax.axis_index("dap")
    sub_index = lax.axis_index("sub")
    alignment_normed = apply_layer_norm(
        homolog_embedding.astype(jnp.float32), homolog_scaling_factor, 2
    ).astype(jnp.bfloat16)
    mask_as_float = alignment_mask.astype(jnp.float32)
    projected_alignment = (
        jnp.einsum(
            "ftv,vy->fty",
            alignment_normed,
            homolog_mapping_matrix,
            preferred_element_type=jnp.float32,
        )
        * mask_as_float[:, :, None]
    )
    left_proj = (
        projected_alignment[:, :, :outer_product_width]
        .astype(jnp.bfloat16)
        .reshape(row_halfway, alignment_row_count * outer_product_width)
    )
    right_proj = (
        projected_alignment[:, :, outer_product_width:]
        .astype(jnp.bfloat16)
        .reshape(row_halfway, alignment_row_count * outer_product_width)
    )
    mask_bits = mask_as_float.astype(jnp.bfloat16)
    left_complete, right_all, mask_all = (
        lax.all_gather(left_proj, "sub", axis=0, tiled=True),
        lax.all_gather(right_proj, "sub", axis=0, tiled=True),
        lax.all_gather(mask_bits, "sub", axis=0, tiled=True),
    )
    packed = jnp.concatenate([right_all, mask_all], axis=1)
    copies = jnp.broadcast_to(packed[None], (lax.axis_size("dap"),) + packed.shape)
    arrived = lax.all_to_all(copies, "dap", split_axis=0, concat_axis=0, tiled=True)
    arrived = jnp.transpose(arrived, (1, 0, 2))
    right_columns = right_all.shape[1]
    right_wide = arrived[:, :, :right_columns].reshape(arrived.shape[0], -1)
    mask_wide = arrived[:, :, right_columns:].reshape(arrived.shape[0], -1)
    right_column_block = lax.dynamic_slice_in_dim(
        right_wide,
        sub_index * (column_halfway * outer_product_width),
        column_halfway * outer_product_width,
        1,
    )
    mask_cols = lax.dynamic_slice_in_dim(mask_wide, sub_index * column_halfway, column_halfway, 1)
    alignment_mask_total = left_complete.shape[0]
    left_row_block = jnp.transpose(
        left_complete.reshape(alignment_mask_total, alignment_row_count, outer_product_width),
        (1, 0, 2),
    )
    right_value_grid = right_column_block.reshape(
        alignment_mask_total, column_halfway, outer_product_width
    )
    counts = jnp.dot(mask_all.T, mask_cols, preferred_element_type=jnp.float32)

    def opm_row(packed):
        left_row, count_row, pair_row = packed
        outer_prod = jnp.einsum(
            "sp,shq->hpq", left_row, right_value_grid, preferred_element_type=jnp.float32
        )
        outer_prod = outer_prod.astype(jnp.bfloat16).reshape(
            column_halfway, outer_product_width * outer_product_width
        )
        values = (
            jnp.dot(outer_prod, outer_output_weight, preferred_element_type=jnp.float32)
            + outer_output_bias
        )
        return (
            pair_row.astype(jnp.float32) + values / jnp.maximum(count_row, 1.0)[:, None]
        ).astype(jnp.bfloat16)

    current = lax.map(opm_row, (left_row_block, counts, pair_activation))
    seq_float = sequence_mask.astype(jnp.float32)
    row_mask = lax.dynamic_slice_in_dim(
        seq_float, dap_index * alignment_row_count, alignment_row_count
    )
    col_mask = lax.dynamic_slice_in_dim(seq_float, sub_index * column_halfway, column_halfway)
    pair_mask = row_mask[:, None] * col_mask[None, :]
    for which in range(2):
        current = triangle(
            current,
            pair_mask,
            pair_norm_gains[2 * which],
            pair_norm_gains[2 * which + 1],
            triangle_input_weights[which],
            triangle_output_weights[which],
            which == 0,
        )
    return current


F32, BF16 = jnp.float32, jnp.bfloat16
MESH = pl.DeviceIdType.MESH
LANES = 128


def dot(a, b, da, db):
    return lax.dot_general(a, b, (((da,), (db,)), ((), ())), preferred_element_type=F32)


def exchange(n, me, source, arrived, send_sem, recv_sem):
    def start(offset, carry):
        peer = lax.rem(me + offset, n)
        pltpu.make_async_remote_copy(
            src_ref=source(peer),
            dst_ref=arrived.at[me],
            send_sem=send_sem,
            recv_sem=recv_sem,
            device_id={"dap": peer},
            device_id_type=MESH,
        ).start()
        return carry

    lax.fori_loop(1, n, start, 0, unroll=True)


def await_bytes(n, arrived, sem):
    others = arrived.at[pl.ds(0, n - 1)]
    pltpu.make_async_copy(others, others, sem).wait()


def fused_kernel(
    n,
    rows,
    depth,
    x_ref,
    mask_ref,
    pair_hbm,
    seq_ref,
    scale_ref,
    map_hbm,
    outer_hbm,
    bias_ref,
    gains_ref,
    w_in_hbm,
    w_out_hbm,
    out_ref,
    recv_a,
    send_b,
    recv_b,
    send_c,
    recv_c,
    wide,
    first,
    second,
    mixed_rows,
    factors,
    w_turned,
    sems,
    gather_sems,
    map_ref,
    outer_ref,
    w_in_ref,
    pair_ref,
    w_out_ref,
    load_sems,
):
    loads = [
        pltpu.make_async_copy(far_away, near, load_sems.at[k])
        for k, (far_away, near) in enumerate(
            (
                (map_hbm, map_ref),
                (w_in_hbm, w_in_ref),
                (outer_hbm, outer_ref),
                (pair_hbm, pair_ref),
                (w_out_hbm, w_out_ref),
            )
        )
    ]
    for load in loads:
        load.start()
    me = lax.axis_index("dap")
    barrier = pltpu.get_barrier_semaphore()

    far, chip, core = me // 8, lax.rem(me // 2, 4), lax.rem(me, 2)
    far_peers = [lax.rem(me + 8 * p, n) for p in range(1, 4)]
    chip_peers = [far * 8 + lax.rem(chip + p, 4) * 2 + core for p in range(1, 4)]
    core_peers = [me + 1 - 2 * core]
    stages = (
        (far_peers, core * 16 + chip * 4 + far, 1),
        (chip_peers, core * 16 + chip * 4, 4),
        (core_peers, core * 16, 16),
    )
    for peer in far_peers + chip_peers + core_peers:
        pl.semaphore_signal(barrier, inc=1, device_id={"dap": peer}, device_id_type=MESH)

    def forward(stage):
        peers, slot, count = stages[stage]
        held = recv_a.at[pl.ds(slot, count)]
        for peer in peers:
            pltpu.make_async_remote_copy(
                src_ref=held,
                dst_ref=held,
                send_sem=gather_sems.at[0, stage],
                recv_sem=gather_sems.at[1, stage],
                device_id={"dap": peer},
                device_id_type=MESH,
            ).start()

    def gathered(stage, way):
        blocks_moved = recv_a.at[pl.ds(0, len(stages[stage][0]) * stages[stage][2])]
        pltpu.make_async_copy(blocks_moved, blocks_moved, gather_sems.at[way, stage]).wait()

    width = pair_ref.shape[2]
    tensor = map_ref.shape[0] // 2
    per = width // n
    strip = rows * per
    blocks = tensor * depth // LANES
    high = tensor // blocks

    normed = apply_layer_norm(x_ref[...].astype(F32), scale_ref[...], 1).astype(BF16)
    mask = jnp.concatenate([mask_ref[...].astype(F32), jnp.zeros((rows, LANES - depth), F32)], axis=1)
    mask = jnp.concatenate([mask, jnp.zeros((LANES - rows, LANES), F32)], axis=0).T
    mask_col = jnp.concatenate([mask[:depth, j : j + 1] for j in range(rows)], axis=0)
    loads[0].wait()
    proj = dot(normed, map_ref[...], 1, 1) * mask_col
    left = proj[:, :tensor].astype(BF16)
    turned = jnp.concatenate(
        [proj, jnp.broadcast_to(mask_col, (rows * depth, LANES - 2 * tensor))], axis=1
    ).T
    pieces = []
    for j in range(rows):
        lanes = slice(j * depth, (j + 1) * depth)
        pieces.append(
            jnp.concatenate(
                [
                    turned[tensor + h * blocks : tensor + (h + 1) * blocks, lanes]
                    for h in range(high)
                ],
                axis=1,
            )
        )
    row_of = lax.broadcasted_iota(jnp.int32, (4 * rows, depth), 0) // 4
    mask_rows = jnp.zeros((4 * rows, depth), F32)
    for j in range(rows):
        spread = turned[2 * tensor : 2 * tensor + 4 * rows, j * depth : (j + 1) * depth]
        mask_rows = jnp.where(row_of == j, spread, mask_rows)
    mask_rows = jnp.concatenate([mask_rows, jnp.zeros((4 * rows, LANES - depth), F32)], axis=1)
    packed = jnp.concatenate(pieces + [mask_rows], axis=0).astype(BF16)
    recv_a[stages[0][1]] = packed
    pl.semaphore_wait(barrier, 7)
    forward(0)

    loads[1].wait()
    for t in range(2):
        w_turned[t] = w_in_ref[t, :, : 4 * width].astype(F32).T.astype(BF16)
    gathered(0, 1)
    forward(1)
    loads[2].wait()
    wide[...] = outer_ref[...].astype(F32)
    for q in range(tensor):
        weight = wide[pl.ds(q, tensor, stride=tensor), :].astype(BF16)
        factor = dot(left, weight, 1, 0).astype(BF16)
        place = (q % blocks) * LANES + (q // blocks) * depth
        for i in range(rows):
            factors[place : place + depth, i * width : (i + 1) * width] = factor[
                i * depth : (i + 1) * depth
            ]
    gathered(1, 1)
    forward(2)
    loads[3].wait()
    loads[4].wait()
    seq = seq_ref[...].astype(F32)
    lane = lax.broadcasted_iota(jnp.int32, seq.shape, 1)
    pair_mask = jnp.concatenate(
        [
            seq * jnp.sum(jnp.where(lane == me * rows + r, seq, 0.0), 1, keepdims=True)
            for r in range(rows)
        ],
        axis=1,
    )

    gathered(2, 1)
    total = n * rows
    kept = rows * blocks
    for d in range(n):
        slot = d % 2 * 16 + d // 2 % 4 * 4 + d // 8
        wide[d * kept : (d + 1) * kept, :] = recv_a[slot, :kept, :].astype(F32)
        first[d * 4 * rows : (d + 1) * 4 * rows, :] = recv_a[slot, kept:, :].astype(F32)
    right = jnp.concatenate(
        [wide[pl.ds(b, total, stride=blocks), :].astype(BF16) for b in range(blocks)], axis=1
    )
    mask_all = first[pl.ds(0, total, stride=4), :][:, :depth].astype(BF16)
    values = dot(right, factors[...], 1, 0)
    current = []
    for i in range(rows):
        own = jnp.broadcast_to(mask_col[i * depth : (i + 1) * depth], (depth, width)).astype(BF16)
        counts = dot(mask_all, own, 1, 0)
        update = (values[:, i * width : (i + 1) * width] + bias_ref[...]) / jnp.maximum(counts, 1.0)
        current.append((pair_ref[i].astype(F32) + update).astype(BF16))

    for t in range(2):
        z = jnp.concatenate([row.astype(F32) for row in current], axis=0)
        normed = apply_layer_norm(z, gains_ref[2 * t : 2 * t + 1, :], 1).astype(BF16)
        turned = dot(w_turned[t], normed, 1, 1)
        for side, scratch in ((0, first), (1, second)):
            value = turned[side * width : (side + 1) * width]
            gate = turned[(2 + side) * width : (3 + side) * width]
            gated = pair_mask * jax.nn.sigmoid(gate) * value
            for r in range(rows):
                scratch[r * width : (r + 1) * width, :] = gated[:, r * total : (r + 1) * total]
            for d in range(n):
                part = slice(side * strip, (side + 1) * strip)
                send_b[t, d, part, :] = scratch[pl.ds(d, strip, stride=n), :].astype(BF16)
        exchange(
            n, me, lambda peer: send_b.at[t, peer], recv_b.at[t], sems.at[t, 0, 0], sems.at[t, 0, 1]
        )
        recv_b[t, me] = send_b[t, me]
        gating = jax.nn.sigmoid(dot(normed, w_in_ref[t, :, 4 * width :], 1, 0))
        gain = jnp.broadcast_to(gains_ref[2 * t + 1 : 2 * t + 2, :], (total, width)).T
        await_bytes(n, recv_b.at[t], sems.at[t, 0, 1])
        first[...] = recv_b[t, :, :strip, :].astype(F32).reshape(n * strip, LANES)
        second[...] = recv_b[t, :, strip:, :].astype(F32).reshape(n * strip, LANES)
        for c in range(per):
            one = first[pl.ds(c, total, stride=per), :].astype(BF16)
            two = second[pl.ds(c, total, stride=per), :].astype(BF16)
            over = 1 - t
            mixed_rows[pl.ds(c, total, stride=per), :] = dot(one, two, over, over)
        send_c[t] = mixed_rows[...].astype(BF16).reshape(n, strip, LANES)
        exchange(n, me, lambda peer: send_c.at[t, peer], recv_c.at[t], sems.at[t, 2, 0], sems.at[t, 2, 1])
        recv_c[t, me] = send_c[t, me]
        await_bytes(n, recv_c.at[t], sems.at[t, 2, 1])
        first[...] = recv_c[t].astype(F32).reshape(n * strip, LANES)
        following = []
        for r in range(rows):
            mixed = jnp.concatenate(
                [first[pl.ds(r * per + c, n, stride=strip), :] for c in range(per)], axis=0
            )
            mixed_norm = apply_layer_norm(mixed, gain, 0).astype(BF16)
            update = dot(mixed_norm, w_out_ref[t], 0, 0)
            block = slice(r * total, (r + 1) * total)
            following.append((z[block] + gating[block] * update).astype(BF16))
        current = following
    for r in range(rows):
        out_ref[r] = current[r]
    for stage in range(3):
        gathered(stage, 0)
    for t in range(2):
        await_bytes(n, recv_b.at[t], sems.at[t, 0, 0])
        await_bytes(n, recv_c.at[t], sems.at[t, 2, 0])


def fused(
    n,
    homolog_embedding,
    alignment_mask,
    pair_activation,
    sequence_mask,
    homolog_scaling_factor,
    homolog_mapping_matrix,
    outer_output_weight,
    outer_output_bias,
    pair_norm_gains,
    triangle_input_weights,
    triangle_output_weights,
):
    depth, rows, channels = homolog_embedding.shape
    total, width = pair_activation.shape[1:]
    strip = rows * (width // n)
    outer = outer_output_weight.shape[0]
    kept = rows * (homolog_mapping_matrix.shape[1] // 2) * depth // LANES
    vmem = pl.BlockSpec(memory_space=pltpu.VMEM)
    hbm = pl.BlockSpec(memory_space=pltpu.HBM)
    return pl.pallas_call(
        functools.partial(fused_kernel, n, rows, depth),
        out_shape=jax.ShapeDtypeStruct(pair_activation.shape, BF16),
        in_specs=[vmem, vmem, hbm, vmem, vmem, hbm, hbm, vmem, vmem, hbm, hbm],
        out_specs=vmem,
        scratch_shapes=[
            pltpu.VMEM((n, kept + 4 * rows, LANES), BF16),
            pltpu.VMEM((2, n, 2 * strip, total), BF16),
            pltpu.VMEM((2, n, 2 * strip, total), BF16),
            pltpu.VMEM((2, n, strip, total), BF16),
            pltpu.VMEM((2, n, strip, total), BF16),
            pltpu.VMEM((outer, width), F32),
            pltpu.VMEM((rows * width, LANES), F32),
            pltpu.VMEM((rows * width, LANES), F32),
            pltpu.VMEM((rows * width, LANES), F32),
            pltpu.VMEM((outer, rows * width), BF16),
            pltpu.VMEM((2, 4 * width, width), BF16),
            pltpu.SemaphoreType.DMA((2, 3, 2)),
            pltpu.SemaphoreType.DMA((2, 3)),
            pltpu.VMEM(homolog_mapping_matrix.shape[::-1], BF16),
            pltpu.VMEM(outer_output_weight.shape, BF16),
            pltpu.VMEM(triangle_input_weights.shape, BF16),
            pltpu.VMEM(pair_activation.shape, BF16),
            pltpu.VMEM(triangle_output_weights.shape, BF16),
            pltpu.SemaphoreType.DMA((5,)),
        ],
        compiler_params=pltpu.CompilerParams(
            collective_id=0, has_side_effects=True, vmem_limit_bytes=62 * 1024 * 1024
        ),
    )(
        jnp.transpose(homolog_embedding, (1, 0, 2)).reshape(rows * depth, channels),
        jnp.transpose(alignment_mask),
        pair_activation,
        sequence_mask.reshape(1, total),
        homolog_scaling_factor.reshape(1, channels),
        jnp.transpose(homolog_mapping_matrix),
        outer_output_weight,
        outer_output_bias.reshape(1, width),
        pair_norm_gains,
        triangle_input_weights,
        triangle_output_weights,
    )


def solution(mesh):
    n, sub = mesh.shape["dap"], mesh.shape["sub"]

    def chosen(*arrays):
        depth, rows, _ = arrays[0].shape
        total, width = arrays[2].shape[1:]
        tensor = arrays[5].shape[1] // 2
        fits = (
            sub == 1
            and (depth, rows, total, width, tensor) == (32, 4, LANES, LANES, 32)
            and n * rows == total
        )
        return fused(n, *arrays) if fits else local(*arrays)
    return jax.shard_map(
        chosen,
        mesh=mesh,
        in_specs=(
            P(("grp", "sub"), "dap", None),
            P(("grp", "sub"), "dap"),
            P(("grp", "dap"), "sub", None),
            P("grp"),
            P(),
            P(),
            P(),
            P(),
            P(),
            P(),
            P(),
        ),
        out_specs=P(("grp", "dap"), "sub", None),
        check_vma=False,
    )
```
